256 devices in a mesh: grp: 8 (over x, y_hi), blk: 32 (over z, y_lo, core).
Axes of the slice: x: 4, y: 4 (y_hi: 2, y_lo: 2; y = y_hi * 2 + y_lo), z: 8, core: 2. Of those that a mesh axis runs over, the one named last changes fastest.
Arguments:
- image_embed: float32 [262144, 768], P(('grp', 'blk')), may hold values from -0.2 to 0.2
- caption_embed: float32 [262144, 768], P(('grp', 'blk')), may hold values from -0.2 to 0.2
- pair_ids: int32 [262144], P(('grp', 'blk')), may hold values from 0 to 262143, as said below
- log_scale: float32 [1], replicated, may hold values from 1 to 2
- logit_bias: float32 [1], replicated, may hold values from -3 to -0.5
Outputs:
- image_grad: float32 [262144, 768], P(('grp', 'blk'))
- caption_grad: float32 [262144, 768], P(('grp', 'blk'))
The draws below stay inside these ranges and needn't reach their ends.
Inputs may be any that keep to these rules, and one draw needn't show every extreme that they name: `pair_ids`: the ids of the rows of each block of 1024 rows are a permutation of that block's own row indices.
All inputs are finite; a program needn't handle non-finite values.
Results may differ from the reference program's by a relative error of at most 0.0003.
Values sent between devices are 32-bit elements; how exact they have to be, the bound alone decides.
No kernel may reach another device: no remote copies, remote signals or barrier semaphores. Data moves between devices by JAX's collectives and lax.ppermute only.
A program may use at most 128 MiB of HBM per device.

```python
import jax
import jax.numpy as jnp
from jax import lax

D = 768
ROWS = 1024
TOKENS = 262144
N_GRP = 8
N_BLK = 32


def draw_pair_ids(key, part):
    key = jax.random.fold_in(key, 7)
    blocks = TOKENS // ROWS
    keys = jax.random.split(key, blocks)
    perms = jax.vmap(lambda k: jax.random.permutation(k, ROWS))(keys).astype(jnp.int32)
    starts = jnp.arange(blocks, dtype=jnp.int32)[:, None] * ROWS
    return (perms + starts).reshape(-1).astype(jnp.int32)


def levels(key, extent, shards, least, high):
    def one(axis_at, parts):
        heights = jax.random.uniform(jax.random.fold_in(jax.random.fold_in(key, 6), axis_at), (parts,), jnp.float32, least / len(shards), high / len(shards))
        return jnp.repeat(jnp.exp(heights), extent[axis_at] // parts).reshape((-1,) + (1,) * (len(extent) - axis_at - 1))

    gain = one(*shards[0])
    for cut in shards[1:]:
        gain = gain * one(*cut)
    return gain


def scatter_about(own_key, shape, width, most, cuts=(), kind=jnp.bfloat16):
    level = levels(own_key, shape, cuts, -0.22, 0.18) if cuts else 1.0
    values = jax.random.normal(own_key, shape, jnp.float32) * width * level
    return jnp.minimum(jnp.maximum(values, -most), most).astype(kind)


def setup_inputs(seed: int = 0) -> dict:
    streams_of = jax.random.split(jax.random.key(seed), 6)
    return {
        "image_embed": scatter_about(streams_of[0], (TOKENS, D), 0.036, 0.2, ((0, 256),), jnp.float32),
        "caption_embed": scatter_about(streams_of[1], (TOKENS, D), 0.036, 0.2, ((0, 256),), jnp.float32),
        "pair_ids": draw_pair_ids(jax.random.fold_in(streams_of[5], 71), 0),
        "log_scale": jnp.clip(jax.random.uniform(streams_of[3], (1,), jnp.float32, 1.0, 2.0), 1.0, 2.0),
        "logit_bias": jnp.clip(jax.random.uniform(streams_of[4], (1,), jnp.float32, -3.0, -0.5), -3.0, -0.5),
    }


def normalize(x):
    n = jnp.sqrt(lax.optimization_barrier(jnp.sum(x * x, axis=-1, keepdims=True)) + 1e-06)
    return (x / n, n)

def block_grads(u, v, ids, cols, scale, bias):
    logits = scale * jnp.dot(u, v.T, precision=lax.Precision.HIGHEST, preferred_element_type=jnp.float32) + bias
    labels = (ids[:, None] == cols[None, :]).astype(jnp.float32)
    g = scale * (jax.nn.sigmoid(logits) - labels)
    du = jnp.dot(g, v, precision=lax.Precision.HIGHEST, preferred_element_type=jnp.float32)
    dv = jnp.dot(g.T, u, precision=lax.Precision.HIGHEST, preferred_element_type=jnp.float32)
    return (du, dv)

def reference(image_embed, caption_embed, pair_ids, log_scale, logit_bias):
    scale = jnp.exp(log_scale[0])
    bias = logit_bias[0]
    u_all, n_img = normalize(image_embed)
    v_all, n_cap = normalize(caption_embed)
    nb = N_GRP * N_BLK
    u_b = u_all.reshape(nb, ROWS, D)
    v_b = v_all.reshape(nb, ROWS, D)
    ids_b = pair_ids.reshape(nb, ROWS)
    local = jnp.arange(ROWS, dtype=jnp.int32)

    def one(d):
        g = d // N_BLK
        k = d % N_BLK
        cycle = g * N_BLK + (k + N_BLK - 1) % N_BLK
        part = (g + N_GRP // 2) % N_GRP * N_BLK + k
        u = u_b[d]
        ids = ids_b[d]
        du0, dv0 = block_grads(u, v_b[d], ids, d * ROWS + local, scale, bias)
        du1, dv1 = block_grads(u, v_b[cycle], ids, cycle * ROWS + local, scale, bias)
        du2, dv2 = block_grads(u, v_b[part], ids, part * ROWS + local, scale, bias)
        return (du0 + du1 + du2, dv0, dv1, dv2)
    du, dv0, dv1, dv2 = lax.map(one, jnp.arange(nb, dtype=jnp.int32))
    dv1 = jnp.roll(dv1.reshape(N_GRP, N_BLK, ROWS, D), -1, axis=1)
    dv2 = jnp.roll(dv2.reshape(N_GRP, N_BLK, ROWS, D), N_GRP // 2, axis=0)
    dv = dv0.reshape(TOKENS, D) + dv1.reshape(TOKENS, D) + dv2.reshape(TOKENS, D)
    du = du.reshape(TOKENS, D)
    image_grad = (du - u_all * lax.optimization_barrier(jnp.sum(u_all * du, axis=-1, keepdims=True))) / n_img
    caption_grad = (dv - v_all * lax.optimization_barrier(jnp.sum(v_all * dv, axis=-1, keepdims=True))) / n_cap
    return (image_grad, caption_grad)
```

```python
import functools

import jax
import jax.numpy as jnp
from jax import lax
from jax.experimental import pallas as pl
from jax.experimental.pallas import tpu as pltpu
from jax.sharding import PartitionSpec as P

EPS = 1e-06
TILE = 256
FIRST = 384
BACK = (768, 960)
VMEM_LIMIT = 52 * 1024 * 1024
NT = (((1,), (1,)), ((), ()))
NN = (((1,), (0,)), ((), ()))
TN = (((0,), (0,)), ((), ()))


def passed_along(block, axis, distance):
    n = lax.axis_size(axis)
    return lax.ppermute(block, axis, [((i - distance) % n, i) for i in range(n)])


def partner(block, axis):
    n = lax.axis_size(axis)
    return lax.ppermute(block, axis, [(i, (i + n // 2) % n) for i in range(n)])


def split(x):
    hi = x.astype(jnp.bfloat16)
    lo = (x - hi.astype(jnp.float32)).astype(jnp.bfloat16)
    return hi, lo


def product(a, b, dims):
    dot = functools.partial(lax.dot_general, dimension_numbers=dims, preferred_element_type=jnp.float32)
    return dot(a[0], b[0]) + (dot(a[0], b[1]) + dot(a[1], b[0]))


def norm_of(x):
    return jnp.sqrt(jnp.sum(x * x, axis=-1, keepdims=True) + EPS)


def weights(u, v, scale, bias, labels):
    weight = jax.nn.sigmoid(scale * product(v, u, NT) + bias)
    if labels is not None:
        weight = weight - labels
    return split(scale * weight)


def score(u, raw, scale, bias, labels):
    v = split(raw * (1.0 / norm_of(raw)))
    g = weights(u, v, scale, bias, labels)
    return product(g, u, NN), product(g, v, TN)


def projected(raw, grad):
    n = norm_of(raw)
    r = 1.0 / n
    unit = raw * r
    return (grad - unit * jnp.sum(unit * grad, axis=-1, keepdims=True)) * r


def captions_kernel(scal_ref, hi_ref, lo_ref, caption_ref, du_in_ref, du_ref):
    @pl.when(pl.program_id(0) == 0)
    def _():
        du_ref[...] = du_in_ref[...]

    v = split(caption_ref[...] * (1.0 / norm_of(caption_ref[...])))
    g = weights((hi_ref[...], lo_ref[...]), v, scal_ref[0], scal_ref[1], None)
    du_ref[...] += product(g, v, TN)


def images_kernel(scal_ref, image_ref, caption_ref, dv_in_ref, dv_ref, hi_ref, lo_ref):
    @pl.when(pl.program_id(0) == 0)
    def _():
        x = image_ref[...]
        hi, lo = split(x * (1.0 / norm_of(x)))
        hi_ref[...] = hi
        lo_ref[...] = lo

    u = (hi_ref[...], lo_ref[...])
    v = split(caption_ref[...] * (1.0 / norm_of(caption_ref[...])))
    g = weights(u, v, scal_ref[0], scal_ref[1], None)
    dv_ref[...] = dv_in_ref[...] + product(g, u, NN)


def own_kernel(first_ref, scal_ref, ids_ref, image_ref, caption_ref, hi_ref, lo_ref, du_ref, dv_ref):
    t = pl.program_id(0)
    tile = caption_ref.shape[0]

    @pl.when(t == 0)
    def _():
        x = image_ref[...]
        hi, lo = split(x * (1.0 / norm_of(x)))
        hi_ref[...] = hi
        lo_ref[...] = lo
        du_ref[...] = jnp.zeros_like(du_ref)

    columns = first_ref[0] + t * tile + lax.broadcasted_iota(jnp.int32, (tile, ids_ref.shape[1]), 0)
    labels = (ids_ref[...] == columns).astype(jnp.float32)
    dv, du = score((hi_ref[...], lo_ref[...]), caption_ref[...], scal_ref[0], scal_ref[1], labels)
    dv_ref[...] = dv
    du_ref[...] += du


def other_kernel(scal_ref, hi_ref, lo_ref, caption_ref, du_in_ref, du_ref, dv_ref):
    t = pl.program_id(0)

    @pl.when(t == 0)
    def _():
        du_ref[...] = du_in_ref[...]

    dv, du = score((hi_ref[...], lo_ref[...]), caption_ref[...], scal_ref[0], scal_ref[1], None)
    dv_ref[...] = dv
    du_ref[...] += du


def last_kernel(scal_ref, hi_ref, lo_ref, caption_ref, du_in_ref, image_ref, grad_ref, dv_ref):
    t = pl.program_id(0)

    @pl.when(t == 0)
    def _():
        grad_ref[...] = du_in_ref[...]

    dv, du = score((hi_ref[...], lo_ref[...]), caption_ref[...], scal_ref[0], scal_ref[1], None)
    dv_ref[...] = dv
    grad_ref[...] += du

    @pl.when(t == pl.num_programs(0) - 1)
    def _():
        grad_ref[...] = projected(image_ref[...], grad_ref[...])


def finish_kernel(caption_ref, base_ref, part_ref, *rest):
    rest[-1][...] = projected(caption_ref[...], base_ref[...] + part_ref[...])


def whole(shape):
    return pl.BlockSpec(shape, lambda t: (0,) * len(shape))


def cost(rows, cols, d):
    return pl.CostEstimate(flops=2 * 9 * rows * cols * d, bytes_accessed=16 * rows * d, transcendentals=0)


SMEM = pl.BlockSpec(memory_space=pltpu.SMEM)
PARAMS = pltpu.CompilerParams(vmem_limit_bytes=VMEM_LIMIT)
SMALL = pltpu.CompilerParams(vmem_limit_bytes=12 * 1024 * 1024)


def own_block(first, scal, ids, image, caption):
    rows, d = image.shape
    tiles = pl.BlockSpec((TILE, d), lambda t: (t, 0))
    return pl.pallas_call(
        own_kernel,
        grid=(rows // TILE,),
        in_specs=[SMEM, SMEM, whole((1, rows)), whole((rows, d)), tiles],
        out_specs=[whole((rows, d)), whole((rows, d)), whole((rows, d)), tiles],
        out_shape=[jax.ShapeDtypeStruct((rows, d), jnp.bfloat16)] * 2 + [jax.ShapeDtypeStruct((rows, d), jnp.float32)] * 2,
        compiler_params=PARAMS,
        cost_estimate=cost(rows, rows, d),
        name='own',
    )(first, scal, ids, image, caption)


def other_block(scal, u, chunk, du, name, image=None):
    rows, d = du.shape
    part = chunk.shape[0]
    tile = max(c for c in range(8, TILE + 128, 8) if part % c == 0)
    tiles = pl.BlockSpec((tile, d), lambda t: (t, 0))
    last = image is not None
    return pl.pallas_call(
        last_kernel if last else other_kernel,
        grid=(part // tile,),
        in_specs=[SMEM, whole((rows, d)), whole((rows, d)), tiles] + [whole((rows, d))] * (1 + last),
        out_specs=[whole((rows, d)), tiles],
        out_shape=[jax.ShapeDtypeStruct((rows, d), jnp.float32), jax.ShapeDtypeStruct((part, d), jnp.float32)],
        compiler_params=PARAMS,
        cost_estimate=cost(part, rows, d),
        name=name,
    )(scal, *u, chunk, du, *([image] if last else []))


def cycle_captions(scal, u, captions, du):
    rows, d = du.shape
    tiles = pl.BlockSpec((TILE, d), lambda t: (t, 0))
    return pl.pallas_call(
        captions_kernel,
        grid=(rows // TILE,),
        in_specs=[SMEM, whole((rows, d)), whole((rows, d)), tiles, whole((rows, d))],
        out_specs=whole((rows, d)),
        out_shape=jax.ShapeDtypeStruct((rows, d), jnp.float32),
        compiler_params=PARAMS,
        cost_estimate=cost(rows, rows, d),
        name='cyc_captions',
    )(scal, *u, captions, du)


def cycle_images(scal, images, captions, dv):
    rows, d = dv.shape
    tiles = pl.BlockSpec((TILE, d), lambda t: (t, 0))
    return pl.pallas_call(
        images_kernel,
        grid=(rows // TILE,),
        in_specs=[SMEM, whole((rows, d)), tiles, tiles],
        out_specs=tiles,
        out_shape=jax.ShapeDtypeStruct((rows, d), jnp.float32),
        scratch_shapes=[pltpu.VMEM((rows, d), jnp.bfloat16)] * 2,
        compiler_params=PARAMS,
        cost_estimate=cost(rows, rows, d),
        name='cyc_images',
    )(scal, images, captions, dv)


def finish(caption, base, part, at, grad=None):
    rows, d = caption.shape
    n = part.shape[0]
    tile = max(c for c in range(8, 200, 8) if n % c == 0 and at % c == 0)
    shifted = pl.BlockSpec((tile, d), lambda t: (t + at // tile, 0))
    more = grad is not None
    return pl.pallas_call(
        finish_kernel,
        grid=(n // tile,),
        in_specs=[shifted, shifted, pl.BlockSpec((tile, d), lambda t: (t, 0))] + [pl.BlockSpec(memory_space=pl.ANY)] * more,
        out_specs=shifted,
        out_shape=jax.ShapeDtypeStruct((rows, d), jnp.float32),
        input_output_aliases={3: 0} if more else {},
        compiler_params=SMALL,
        cost_estimate=cost(1, 1, 1),
    )(caption, base, part, *([grad] if more else []))


def body(image_embed, caption_embed, pair_ids, log_scale, logit_bias):
    rows = image_embed.shape[0]
    chunk0, later = lax.optimization_barrier((caption_embed[:FIRST], caption_embed))
    part0 = partner(chunk0, "grp")
    part1 = partner(later[FIRST:], "grp")
    cyc_captions = passed_along(caption_embed, "blk", 1)
    cyc_images = passed_along(image_embed, "blk", -1)
    scal = jnp.concatenate([jnp.exp(log_scale), logit_bias])
    first = (lax.axis_index("grp") * lax.axis_size("blk") + lax.axis_index("blk")) * rows
    hi, lo, du, dv_own = own_block(first.astype(jnp.int32)[None], scal, pair_ids[None, :], image_embed, caption_embed)
    u = (hi, lo)
    du, dv_part0 = other_block(scal, u, part0, du, "part_a")
    back0 = partner(dv_part0, "grp")
    du = cycle_captions(scal, u, cyc_captions, du)
    image_grad, dv_part1 = other_block(scal, u, part1, du, "part_b", image_embed)
    dv_part1, cyc_images = lax.optimization_barrier((dv_part1, cyc_images))
    base = cycle_images(scal, cyc_images, caption_embed, dv_own)
    grad = finish(caption_embed, base, back0, 0)
    edges = (FIRST,) + BACK + (rows,)
    for lo_row, hi_row in zip(edges, edges[1:]):
        back = partner(dv_part1[lo_row - FIRST : hi_row - FIRST], "grp")
        grad = finish(caption_embed, base, back, lo_row, grad)
    return (image_grad, grad)


def solution(mesh):
    in_specs = (P(("grp", "blk"), None), P(("grp", "blk"), None), P(("grp", "blk")), P(), P())
    out_specs = (P(("grp", "blk"), None), P(("grp", "blk"), None))
    return jax.shard_map(body, mesh=mesh, in_specs=in_specs, out_specs=out_specs, check_vma=False)
```

```python
import functools

import jax
import jax.numpy as jnp
from jax import lax
from jax.experimental import pallas as pl
from jax.experimental.pallas import tpu as pltpu
from jax.sharding import PartitionSpec as P

EPS = 1e-06
TILE = 256
FIRST = 384
SCALE = dict(own=1.0, part_a=1.0, cyc_captions=1.0, part_b=2.0)
BACK = (768, 960)
NT = (((1,), (1,)), ((), ()))
NN = (((1,), (0,)), ((), ()))
TN = (((0,), (0,)), ((), ()))
F32 = jnp.float32
SMEM = pl.BlockSpec(memory_space=pltpu.SMEM)
PARAMS = pltpu.CompilerParams(vmem_limit_bytes=52 * 1024 * 1024)
SMALL = pltpu.CompilerParams(vmem_limit_bytes=12 * 1024 * 1024)


def passed_along(block, axis, distance):
    n = lax.axis_size(axis)
    return lax.ppermute(block, axis, [((i - distance) % n, i) for i in range(n)])


def partner(block, axis):
    n = lax.axis_size(axis)
    return lax.ppermute(block, axis, [(i, (i + n // 2) % n) for i in range(n)])


def split(x):
    hi = x.astype(jnp.bfloat16)
    lo = (x - hi.astype(F32)).astype(jnp.bfloat16)
    return hi, lo


def product(a, b, dims):
    dot = functools.partial(lax.dot_general, dimension_numbers=dims, preferred_element_type=F32)
    return dot(a[0], b[0]) + (dot(a[0], b[1]) + dot(a[1], b[0]))


def norm_of(x):
    return jnp.sqrt(jnp.sum(x * x, axis=-1, keepdims=True) + EPS)


def unit(x):
    return x * (1.0 / norm_of(x))


def projected(raw, grad):
    r = 1.0 / norm_of(raw)
    one = raw * r
    return (grad - one * jnp.sum(one * grad, axis=-1, keepdims=True)) * r


def weights(u, v, scal_ref, labels=None):
    weight = jax.nn.sigmoid(scal_ref[0] * product(v, u, NT) + scal_ref[1])
    if labels is not None:
        weight = weight - labels
    return split(scal_ref[0] * weight)


def own_kernel(first_ref, scal_ref, ids_ref, image_ref, caption_ref, u_ref, du_ref, dv_ref, hi_ref, lo_ref):
    t = pl.program_id(0)
    tile = caption_ref.shape[0]

    @pl.when(t == 0)
    def _():
        u = unit(image_ref[...])
        u_ref[...] = u
        hi_ref[...], lo_ref[...] = split(u)
        du_ref[...] = jnp.zeros_like(du_ref)

    columns = first_ref[0] + t * tile + lax.broadcasted_iota(jnp.int32, (tile, ids_ref.shape[1]), 0)
    labels = (ids_ref[...] == columns).astype(F32)
    u = (hi_ref[...], lo_ref[...])
    v = split(unit(caption_ref[...]))
    g = weights(u, v, scal_ref, labels)
    dv_ref[...] = product(g, u, NN)
    du_ref[...] += product(g, v, TN)


def score_kernel(chunks, tile, scal_ref, u_ref, *rest):
    caption_refs, (du_in_ref, du_ref), dv_refs = rest[:chunks], rest[chunks : chunks + 2], rest[chunks + 2 : -4]
    hi_ref, lo_ref, v_hi_ref, v_lo_ref = rest[-4:]
    t = pl.program_id(0)

    @pl.when(t == 0)
    def _():
        hi_ref[...], lo_ref[...] = split(u_ref[...])
        at = 0
        for ref in caption_refs:
            n = ref.shape[0]
            v_hi_ref[at : at + n, :], v_lo_ref[at : at + n, :] = split(unit(ref[...]))
            at += n
        du_ref[...] = du_in_ref[...]

    rows = pl.ds(pl.multiple_of(t * tile, 64), tile)
    u = (hi_ref[...], lo_ref[...])
    v = (v_hi_ref[rows, :], v_lo_ref[rows, :])
    g = weights(u, v, scal_ref)
    if dv_refs:
        dv = product(g, u, NN)
        for step in range(v_hi_ref.shape[0] // tile):

            @pl.when(t == step)
            def _():
                at = 0
                for ref in dv_refs:
                    a, b = max(at, step * tile), min(at + ref.shape[0], (step + 1) * tile)
                    if a < b:
                        ref[a - at : b - at, :] = dv[a - step * tile : b - step * tile, :]
                    at += ref.shape[0]

    du_ref[...] += product(g, v, TN)


def images_kernel(scal_ref, u_ref, caption_ref, dv_in_ref, dv_ref, hi_ref, lo_ref):
    @pl.when(pl.program_id(0) == 0)
    def _():
        hi_ref[...], lo_ref[...] = split(u_ref[...])

    u = (hi_ref[...], lo_ref[...])
    g = weights(u, split(unit(caption_ref[...])), scal_ref)
    dv_ref[...] = dv_in_ref[...] + product(g, u, NN)


def image_kernel(image_ref, du_ref, grad_ref):
    grad_ref[...] = projected(image_ref[...], du_ref[...])


def finish_kernel(caption_ref, base_ref, part_ref, *rest):
    rest[-1][...] = projected(caption_ref[...], base_ref[...] + part_ref[...])


def whole(shape):
    return pl.BlockSpec(shape, lambda t: (0,) * len(shape))


def blocks(tile, d, first=0):
    return pl.BlockSpec((tile, d), lambda t: (t + first, 0))


def shape(rows, d):
    return jax.ShapeDtypeStruct((rows, d), F32)


def halves(rows, d):
    return [pltpu.VMEM((rows, d), jnp.bfloat16)] * 2


def cost(products, rows, cols, d, scale=1.0):
    return pl.CostEstimate(flops=int(scale * 2 * 3 * products * rows * cols * d), bytes_accessed=16 * rows * d, transcendentals=rows * cols)


def own_block(first, scal, ids, image, caption):
    rows, d = image.shape
    return pl.pallas_call(
        own_kernel,
        grid=(rows // TILE,),
        in_specs=[SMEM, SMEM, whole((1, rows)), whole((rows, d)), blocks(TILE, d)],
        out_specs=[whole((rows, d)), whole((rows, d)), blocks(TILE, d)],
        out_shape=[shape(rows, d)] * 3,
        scratch_shapes=halves(rows, d),
        compiler_params=PARAMS,
        cost_estimate=cost(3, rows, rows, d, SCALE['own']),
        name="own",
    )(first, scal, ids, image, caption)


def score(scal, u, chunks, du, pieces, name):
    rows, d = u.shape
    part = sum(c.shape[0] for c in chunks)
    tile = max(c for c in range(64, TILE + 128, 64) if part % c == 0)
    return pl.pallas_call(
        functools.partial(score_kernel, len(chunks), tile),
        grid=(part // tile,),
        in_specs=[SMEM, whole((rows, d))] + [whole(c.shape) for c in chunks] + [whole((rows, d))],
        out_specs=[whole((rows, d))] + [whole((n, d)) for n in pieces],
        out_shape=[shape(rows, d)] + [shape(n, d) for n in pieces],
        scratch_shapes=halves(rows, d) + halves(part, d),
        compiler_params=PARAMS,
        cost_estimate=cost(3 if pieces else 2, part, rows, d, SCALE[name]),
        name=name,
    )(scal, u, *chunks, du)


def cycle_images(scal, u, caption, dv):
    rows, d = dv.shape
    return pl.pallas_call(
        images_kernel,
        grid=(rows // TILE,),
        in_specs=[SMEM, whole((rows, d)), blocks(TILE, d), blocks(TILE, d)],
        out_specs=blocks(TILE, d),
        out_shape=shape(rows, d),
        scratch_shapes=halves(rows, d),
        compiler_params=PARAMS,
        cost_estimate=cost(2, rows, rows, d),
        name="cyc_images",
    )(scal, u, caption, dv)


def image_finish(image, du):
    rows, d = du.shape
    return pl.pallas_call(
        image_kernel,
        grid=(rows // TILE,),
        in_specs=[blocks(TILE, d)] * 2,
        out_specs=blocks(TILE, d),
        out_shape=shape(rows, d),
        compiler_params=SMALL,
        cost_estimate=pl.CostEstimate(flops=10 * du.size, bytes_accessed=12 * du.size, transcendentals=0),
        name="image_grad",
    )(image, du)


def finish(caption, base, part, at, grad=None):
    rows, d = caption.shape
    n = part.shape[0]
    tile = max(c for c in range(8, 200, 8) if n % c == 0 and at % c == 0)
    more = grad is not None
    return pl.pallas_call(
        finish_kernel,
        grid=(n // tile,),
        in_specs=[blocks(tile, d, at // tile)] * 2 + [blocks(tile, d)] + [pl.BlockSpec(memory_space=pl.ANY)] * more,
        out_specs=blocks(tile, d, at // tile),
        out_shape=shape(rows, d),
        input_output_aliases={3: 0} if more else {},
        compiler_params=SMALL,
        cost_estimate=pl.CostEstimate(flops=10 * part.size, bytes_accessed=16 * part.size, transcendentals=0),
        name="finish",
    )(caption, base, part, *([grad] if more else []))


def body(image_embed, caption_embed, pair_ids, log_scale, logit_bias):
    rows = image_embed.shape[0]
    chunk0, later = lax.optimization_barrier((caption_embed[:FIRST], caption_embed))
    chunk1 = later[FIRST:]
    part0, part1 = (partner(c, "grp") for c in (chunk0, chunk1))
    cycle0, cycle1 = (passed_along(c, "blk", 1) for c in (chunk0, chunk1))
    scal = jnp.concatenate([jnp.exp(log_scale), logit_bias])
    first = (lax.axis_index("grp") * lax.axis_size("blk") + lax.axis_index("blk")) * rows
    u, du, dv = own_block(first.astype(jnp.int32)[None], scal, pair_ids[None, :], image_embed, caption_embed)
    next_u = passed_along(u, "blk", -1)
    du, dv_part0 = score(scal, u, [part0], du, [FIRST], "part_a")
    back0 = partner(dv_part0, "grp")
    (du,) = score(scal, u, [cycle0, cycle1], du, [], "cyc_captions")
    edges = (FIRST,) + BACK + (rows,)
    pieces = [b - a for a, b in zip(edges, edges[1:])]
    du, *dv_part1 = score(scal, u, [part1], du, pieces, "part_b")
    backs = [partner(piece, "grp") for piece in dv_part1]
    base = cycle_images(scal, next_u, caption_embed, dv)
    image_grad = image_finish(image_embed, du)
    grad = finish(caption_embed, base, back0, 0)
    for at, back in zip(edges, backs):
        grad = finish(caption_embed, base, back, at, grad)
    return (image_grad, grad)


def solution(mesh):
    in_specs = (P(("grp", "blk"), None), P(("grp", "blk"), None), P(("grp", "blk")), P(), P())
    out_specs = (P(("grp", "blk"), None), P(("grp", "blk"), None))
    return jax.shard_map(body, mesh=mesh, in_specs=in_specs, out_specs=out_specs, check_vma=False)
```

```python
import functools

import jax
import jax.numpy as jnp
from jax import lax
from jax.experimental import pallas as pl
from jax.experimental.pallas import tpu as pltpu
from jax.sharding import PartitionSpec as P

EPS = 1e-06
TILE = 256
CUTS = (384,)
SCALE = dict(own=1.0, part_a=1.0, cyc_captions=1.0, part_b=2.0)
BACK = (768, 960)
NT = (((1,), (1,)), ((), ()))
NN = (((1,), (0,)), ((), ()))
TN = (((0,), (0,)), ((), ()))
F32 = jnp.float32
SMEM = pl.BlockSpec(memory_space=pltpu.SMEM)
PARAMS = pltpu.CompilerParams(vmem_limit_bytes=52 * 1024 * 1024)
SMALL = pltpu.CompilerParams(vmem_limit_bytes=12 * 1024 * 1024)


def passed_along(block, axis, distance):
    n = lax.axis_size(axis)
    return lax.ppermute(block, axis, [((i - distance) % n, i) for i in range(n)])


def partner(block, axis):
    n = lax.axis_size(axis)
    return lax.ppermute(block, axis, [(i, (i + n // 2) % n) for i in range(n)])


def split(x):
    hi = x.astype(jnp.bfloat16)
    lo = (x - hi.astype(F32)).astype(jnp.bfloat16)
    return hi, lo


def product(a, b, dims):
    dot = functools.partial(lax.dot_general, dimension_numbers=dims, preferred_element_type=F32)
    return dot(a[0], b[0]) + (dot(a[0], b[1]) + dot(a[1], b[0]))


def norm_of(x):
    return jnp.sqrt(jnp.sum(x * x, axis=-1, keepdims=True) + EPS)


def unit(x):
    return x * (1.0 / norm_of(x))


def projected(raw, grad):
    r = 1.0 / norm_of(raw)
    one = raw * r
    return (grad - one * jnp.sum(one * grad, axis=-1, keepdims=True)) * r


def weights(u, v, scal_ref, labels=None):
    weight = jax.nn.sigmoid(scal_ref[0] * product(v, u, NT) + scal_ref[1])
    if labels is not None:
        weight = weight - labels
    return split(scal_ref[0] * weight)


def own_kernel(first_ref, scal_ref, ids_ref, image_ref, caption_ref, u_ref, hi_ref, lo_ref, du_ref, dv_ref):
    t = pl.program_id(0)
    tile = caption_ref.shape[0]

    @pl.when(t == 0)
    def _():
        u = unit(image_ref[...])
        u_ref[...] = u
        hi_ref[...], lo_ref[...] = split(u)
        du_ref[...] = jnp.zeros_like(du_ref)

    columns = first_ref[0] + t * tile + lax.broadcasted_iota(jnp.int32, (tile, ids_ref.shape[1]), 0)
    labels = (ids_ref[...] == columns).astype(F32)
    u = (hi_ref[...], lo_ref[...])
    v = split(unit(caption_ref[...]))
    g = weights(u, v, scal_ref, labels)
    dv_ref[...] = product(g, u, NN)
    du_ref[...] += product(g, v, TN)


def score_kernel(chunks, passed, tile, scal_ref, hi_ref, lo_ref, *rest):
    caption_refs, du_in_ref, du_ref = rest[:chunks], rest[chunks], rest[chunks + 1 + passed]
    dv_refs, (v_hi_ref, v_lo_ref) = rest[chunks + 2 + 2 * passed : -2], rest[-2:]
    t = pl.program_id(0)

    @pl.when(t == 0)
    def _():
        at = 0
        for ref in caption_refs:
            n = ref.shape[0]
            v_hi_ref[at : at + n, :], v_lo_ref[at : at + n, :] = split(unit(ref[...]))
            at += n
        du_ref[...] = du_in_ref[...]

    rows = pl.ds(pl.multiple_of(t * tile, 64), tile)
    u = (hi_ref[...], lo_ref[...])
    v = (v_hi_ref[rows, :], v_lo_ref[rows, :])
    g = weights(u, v, scal_ref)
    if dv_refs:
        dv = product(g, u, NN)
        for step in range(v_hi_ref.shape[0] // tile):

            @pl.when(t == step)
            def _():
                at = 0
                for ref in dv_refs:
                    a, b = max(at, step * tile), min(at + ref.shape[0], (step + 1) * tile)
                    if a < b:
                        ref[a - at : b - at, :] = dv[a - step * tile : b - step * tile, :]
                    at += ref.shape[0]

    du_ref[...] += product(g, v, TN)


def images_kernel(scal_ref, u_ref, caption_ref, dv_in_ref, dv_ref, hi_ref, lo_ref):
    @pl.when(pl.program_id(0) == 0)
    def _():
        hi_ref[...], lo_ref[...] = split(u_ref[...])

    u = (hi_ref[...], lo_ref[...])
    g = weights(u, split(unit(caption_ref[...])), scal_ref)
    dv_ref[...] = dv_in_ref[...] + product(g, u, NN)


def image_kernel(image_ref, du_ref, grad_ref):
    grad_ref[...] = projected(image_ref[...], du_ref[...])


def finish_kernel(caption_ref, base_ref, part_ref, *rest):
    rest[-1][...] = projected(caption_ref[...], base_ref[...] + part_ref[...])


def whole(shape):
    return pl.BlockSpec(shape, lambda t: (0,) * len(shape))


def blocks(tile, d, first=0):
    return pl.BlockSpec((tile, d), lambda t: (t + first, 0))


def shape(rows, d, dtype=F32):
    return jax.ShapeDtypeStruct((rows, d), dtype)


def halves(rows, d):
    return [pltpu.VMEM((rows, d), jnp.bfloat16)] * 2


def cost(products, rows, cols, d, scale=1.0):
    return pl.CostEstimate(flops=int(scale * 2 * 3 * products * rows * cols * d), bytes_accessed=16 * rows * d, transcendentals=rows * cols)


def own_block(first, scal, ids, image, caption):
    rows, d = image.shape
    return pl.pallas_call(
        own_kernel,
        grid=(rows // TILE,),
        in_specs=[SMEM, SMEM, whole((1, rows)), whole((rows, d)), blocks(TILE, d)],
        out_specs=[whole((rows, d))] * 4 + [blocks(TILE, d)],
        out_shape=[shape(rows, d)] + [shape(rows, d, jnp.bfloat16)] * 2 + [shape(rows, d)] * 2,
        compiler_params=PARAMS,
        cost_estimate=cost(3, rows, rows, d, SCALE['own']),
        name="own",
    )(first, scal, ids, image, caption)


def score(scal, u, chunks, du, pieces, name, passed=None):
    rows, d = du.shape
    part = sum(c.shape[0] for c in chunks)
    tile = max(c for c in range(64, TILE + 128, 64) if part % c == 0)
    extra = [] if passed is None else [passed]
    kept = [pl.BlockSpec(memory_space=pl.ANY)] * len(extra)
    return pl.pallas_call(
        functools.partial(score_kernel, len(chunks), len(extra), tile),
        grid=(part // tile,),
        in_specs=[SMEM] + [whole((rows, d))] * 2 + [whole(c.shape) for c in chunks] + [whole((rows, d))] + kept,
        out_specs=[whole((rows, d))] + kept + [whole((n, d)) for n in pieces],
        out_shape=[shape(rows, d)] + [shape(*x.shape) for x in extra] + [shape(n, d) for n in pieces],
        scratch_shapes=halves(part, d),
        input_output_aliases={4 + len(chunks): 1} if extra else {},
        compiler_params=PARAMS,
        cost_estimate=cost(3 if pieces else 2, part, rows, d, SCALE[name]),
        name=name,
    )(scal, *u, *chunks, du, *extra)


def cycle_images(scal, u, caption, dv):
    rows, d = dv.shape
    return pl.pallas_call(
        images_kernel,
        grid=(rows // TILE,),
        in_specs=[SMEM, whole((rows, d)), blocks(TILE, d), blocks(TILE, d)],
        out_specs=blocks(TILE, d),
        out_shape=shape(rows, d),
        scratch_shapes=halves(rows, d),
        compiler_params=PARAMS,
        cost_estimate=cost(2, rows, rows, d),
        name="cyc_images",
    )(scal, u, caption, dv)


def image_finish(image, du):
    rows, d = du.shape
    return pl.pallas_call(
        image_kernel,
        grid=(rows // TILE,),
        in_specs=[blocks(TILE, d)] * 2,
        out_specs=blocks(TILE, d),
        out_shape=shape(rows, d),
        compiler_params=SMALL,
        cost_estimate=pl.CostEstimate(flops=10 * du.size, bytes_accessed=12 * du.size, transcendentals=0),
        name="image_grad",
    )(image, du)


def finish(caption, base, part, at, grad=None):
    rows, d = caption.shape
    n = part.shape[0]
    tile = max(c for c in range(8, 200, 8) if n % c == 0 and at % c == 0)
    more = grad is not None
    return pl.pallas_call(
        finish_kernel,
        grid=(n // tile,),
        in_specs=[blocks(tile, d, at // tile)] * 2 + [blocks(tile, d)] + [pl.BlockSpec(memory_space=pl.ANY)] * more,
        out_specs=blocks(tile, d, at // tile),
        out_shape=shape(rows, d),
        input_output_aliases={3: 0} if more else {},
        compiler_params=SMALL,
        cost_estimate=pl.CostEstimate(flops=10 * part.size, bytes_accessed=16 * part.size, transcendentals=0),
        name="finish",
    )(caption, base, part, *([grad] if more else []))


def body(image_embed, caption_embed, pair_ids, log_scale, logit_bias):
    rows = image_embed.shape[0]
    chunks, later = [], caption_embed
    for a, b in zip((0,) + CUTS, CUTS + (rows,)):
        chunk, later = lax.optimization_barrier((later[a:b], later))
        chunks.append(chunk)
    parts = [partner(c, "grp") for c in chunks]
    cycles = [passed_along(c, "blk", 1) for c in chunks]
    scal = jnp.concatenate([jnp.exp(log_scale), logit_bias])
    first = (lax.axis_index("grp") * lax.axis_size("blk") + lax.axis_index("blk")) * rows
    one, hi, lo, du, dv = own_block(first.astype(jnp.int32)[None], scal, pair_ids[None, :], image_embed, caption_embed)
    u = (hi, lo)
    du, one, dv_part0 = score(scal, u, parts[:-1], du, [CUTS[-1]], "part_a", one)
    back0 = partner(dv_part0, "grp")
    next_u = passed_along(one, "blk", -1)
    (du,) = score(scal, u, cycles, du, [], "cyc_captions")
    edges = CUTS[-1:] + BACK + (rows,)
    pieces = [b - a for a, b in zip(edges, edges[1:])]
    du, *dv_part1 = score(scal, u, parts[-1:], du, pieces, "part_b")
    backs = [partner(piece, "grp") for piece in dv_part1]
    base = cycle_images(scal, next_u, caption_embed, dv)
    image_grad = image_finish(image_embed, du)
    grad = finish(caption_embed, base, back0, 0)
    for at, back in zip(edges, backs):
        grad = finish(caption_embed, base, back, at, grad)
    return (image_grad, grad)


def solution(mesh):
    in_specs = (P(("grp", "blk"), None), P(("grp", "blk"), None), P(("grp", "blk")), P(), P())
    out_specs = (P(("grp", "blk"), None), P(("grp", "blk"), None))
    return jax.shard_map(body, mesh=mesh, in_specs=in_specs, out_specs=out_specs, check_vma=False)
```

```python
import functools

import jax
import jax.numpy as jnp
from jax import lax
from jax.experimental import pallas as pl
from jax.experimental.pallas import tpu as pltpu
from jax.sharding import PartitionSpec as P

EPS = 1e-06
TILE = 256
VMEM = 42
CUTS = (320,)
SCALE = dict(own=1.0, part_a=1.0, cyc_captions=1.0, part_b=2.0, rest=0.5)
BACK = (640, 832, 960)
NT = (((1,), (1,)), ((), ()))
NN = (((1,), (0,)), ((), ()))
TN = (((0,), (0,)), ((), ()))
F32 = jnp.float32
SMEM = pl.BlockSpec(memory_space=pltpu.SMEM)
PARAMS = pltpu.CompilerParams(vmem_limit_bytes=VMEM * 1024 * 1024)
SMALL = pltpu.CompilerParams(vmem_limit_bytes=12 * 1024 * 1024)


def passed_along(block, axis, distance):
    n = lax.axis_size(axis)
    return lax.ppermute(block, axis, [((i - distance) % n, i) for i in range(n)])


def partner(block, axis):
    n = lax.axis_size(axis)
    return lax.ppermute(block, axis, [(i, (i + n // 2) % n) for i in range(n)])


def split(x):
    hi = x.astype(jnp.bfloat16)
    lo = (x - hi.astype(F32)).astype(jnp.bfloat16)
    return hi, lo


def product(a, b, dims):
    dot = functools.partial(lax.dot_general, dimension_numbers=dims, preferred_element_type=F32)
    return dot(a[0], b[0]) + (dot(a[0], b[1]) + dot(a[1], b[0]))


def norm_of(x):
    return jnp.sqrt(jnp.sum(x * x, axis=-1, keepdims=True) + EPS)


def unit(x):
    return x * (1.0 / norm_of(x))


def projected(raw, grad):
    r = 1.0 / norm_of(raw)
    one = raw * r
    return (grad - one * jnp.sum(one * grad, axis=-1, keepdims=True)) * r


def weights(u, v, scal_ref, labels=None):
    weight = jax.nn.sigmoid(scal_ref[0] * product(v, u, NT) + scal_ref[1])
    if labels is not None:
        weight = weight - labels
    return split(scal_ref[0] * weight)


def cut_kernel(first, x_ref, out_ref, sems):
    step = out_ref.shape[0] // sems.shape[0]
    copies = []
    for i in range(sems.shape[0]):
        source = x_ref.at[pl.ds(first + i * step, step), :]
        copies.append(pltpu.make_async_copy(source, out_ref.at[pl.ds(i * step, step), :], sems.at[i]))
        copies[-1].start()
    for copy in copies:
        copy.wait()


def own_kernel(first_ref, scal_ref, ids_ref, image_ref, caption_ref, u_ref, hi_ref, lo_ref, du_ref, dv_ref):
    t = pl.program_id(0)
    tile = caption_ref.shape[0]

    @pl.when(t == 0)
    def _():
        u = unit(image_ref[...])
        u_ref[...] = u
        hi_ref[...], lo_ref[...] = split(u)
        du_ref[...] = jnp.zeros_like(du_ref)

    columns = first_ref[0] + t * tile + lax.broadcasted_iota(jnp.int32, (tile, ids_ref.shape[1]), 0)
    labels = (ids_ref[...] == columns).astype(F32)
    u = (hi_ref[...], lo_ref[...])
    v = split(unit(caption_ref[...]))
    g = weights(u, v, scal_ref, labels)
    dv_ref[...] = product(g, u, NN)
    du_ref[...] += product(g, v, TN)


def score_kernel(chunks, passed, tile, scal_ref, hi_ref, lo_ref, *rest):
    caption_refs, du_in_ref, du_ref = rest[:chunks], rest[chunks], rest[chunks + 1 + passed]
    dv_refs, (v_hi_ref, v_lo_ref) = rest[chunks + 2 + 2 * passed : -2], rest[-2:]
    t = pl.program_id(0)

    @pl.when(t == 0)
    def _():
        at = 0
        for ref in caption_refs:
            n = ref.shape[0]
            v_hi_ref[at : at + n, :], v_lo_ref[at : at + n, :] = split(unit(ref[...]))
            at += n
        du_ref[...] = du_in_ref[...]

    rows = pl.ds(pl.multiple_of(t * tile, 16), tile)
    u = (hi_ref[...], lo_ref[...])
    v = (v_hi_ref[rows, :], v_lo_ref[rows, :])
    g = weights(u, v, scal_ref)
    if dv_refs:
        dv = product(g, u, NN)
        for step in range(v_hi_ref.shape[0] // tile):

            @pl.when(t == step)
            def _():
                at = 0
                for ref in dv_refs:
                    a, b = max(at, step * tile), min(at + ref.shape[0], (step + 1) * tile)
                    if a < b:
                        ref[a - at : b - at, :] = dv[a - step * tile : b - step * tile, :]
                    at += ref.shape[0]

    du_ref[...] += product(g, v, TN)


def returns_kernel(tile, scal_ref, hi_ref, lo_ref, caption_ref, after_ref, g_hi_ref, g_lo_ref, v_hi_ref, v_lo_ref, *dv_refs):
    del after_ref
    t = pl.program_id(0)
    u = (hi_ref[...], lo_ref[...])
    v = split(unit(caption_ref[...]))
    v_hi_ref[...], v_lo_ref[...] = v
    g = weights(u, v, scal_ref)
    g_hi_ref[...], g_lo_ref[...] = g
    dv = product(g, u, NN)
    for step in range(sum(ref.shape[0] for ref in dv_refs) // tile):

        @pl.when(t == step)
        def _():
            at = 0
            for ref in dv_refs:
                a, b = max(at, step * tile), min(at + ref.shape[0], (step + 1) * tile)
                if a < b:
                    ref[a - at : b - at, :] = dv[a - step * tile : b - step * tile, :]
                at += ref.shape[0]


def rest_kernel(g_hi_ref, g_lo_ref, v_hi_ref, v_lo_ref, du_ref, image_ref, grad_ref):
    du = du_ref[...] + product((g_hi_ref[...], g_lo_ref[...]), (v_hi_ref[...], v_lo_ref[...]), TN)
    grad_ref[...] = projected(image_ref[...], du)


def images_kernel(scal_ref, u_ref, caption_ref, dv_in_ref, dv_ref, hi_ref, lo_ref):
    @pl.when(pl.program_id(0) == 0)
    def _():
        hi_ref[...], lo_ref[...] = split(u_ref[...])

    u = (hi_ref[...], lo_ref[...])
    g = weights(u, split(unit(caption_ref[...])), scal_ref)
    dv_ref[...] = dv_in_ref[...] + product(g, u, NN)


def finish_kernel(caption_ref, base_ref, part_ref, *rest):
    rest[-1][...] = projected(caption_ref[...], base_ref[...] + part_ref[...])


def whole(shape):
    return pl.BlockSpec(shape, lambda t: (0,) * len(shape), pipeline_mode=pl.Buffered(1))


def result(shape):
    return pl.BlockSpec(shape, lambda t: (0,) * len(shape))


def blocks(tile, d, first=0):
    return pl.BlockSpec((tile, d), lambda t: (t + first, 0))


def shape(rows, d, dtype=F32):
    return jax.ShapeDtypeStruct((rows, d), dtype)


def halves(rows, d):
    return [pltpu.VMEM((rows, d), jnp.bfloat16)] * 2


def cost(products, rows, cols, d, scale=1.0):
    return pl.CostEstimate(flops=int(scale * 2 * 3 * products * rows * cols * d), bytes_accessed=16 * rows * d, transcendentals=rows * cols)


def cut(x, first, last):
    n, d = last - first, x.shape[1]
    return pl.pallas_call(
        functools.partial(cut_kernel, first),
        in_specs=[pl.BlockSpec(memory_space=pl.ANY)],
        out_specs=pl.BlockSpec(memory_space=pl.ANY),
        out_shape=shape(n, d),
        scratch_shapes=[pltpu.SemaphoreType.DMA((8,))],
        compiler_params=pltpu.CompilerParams(vmem_limit_bytes=60 * 1024 * 1024),
        cost_estimate=pl.CostEstimate(flops=0, bytes_accessed=8 * n * d, transcendentals=0),
        name="cut",
    )(x)


def own_block(first, scal, ids, image, caption):
    rows, d = image.shape
    return pl.pallas_call(
        own_kernel,
        grid=(rows // TILE,),
        in_specs=[SMEM, SMEM, whole((1, rows)), whole((rows, d)), blocks(TILE, d)],
        out_specs=[result((rows, d))] * 4 + [blocks(TILE, d)],
        out_shape=[shape(rows, d)] + [shape(rows, d, jnp.bfloat16)] * 2 + [shape(rows, d)] * 2,
        compiler_params=PARAMS,
        cost_estimate=cost(3, rows, rows, d, SCALE['own']),
        name="own",
    )(first, scal, ids, image, caption)


def score(scal, u, chunks, du, pieces, name, passed=None):
    rows, d = du.shape
    part = sum(c.shape[0] for c in chunks)
    tile = max(c for c in range(16, TILE + 128, 16) if part % c == 0)
    extra = [] if passed is None else [passed]
    kept = [pl.BlockSpec(memory_space=pl.ANY)] * len(extra)
    return pl.pallas_call(
        functools.partial(score_kernel, len(chunks), len(extra), tile),
        grid=(part // tile,),
        in_specs=[SMEM] + [whole((rows, d))] * 2 + [whole(c.shape) for c in chunks] + [whole((rows, d))] + kept,
        out_specs=[result((rows, d))] + kept + [result((n, d)) for n in pieces],
        out_shape=[shape(rows, d)] + [shape(*x.shape) for x in extra] + [shape(n, d) for n in pieces],
        scratch_shapes=halves(part, d),
        input_output_aliases={4 + len(chunks): 1} if extra else {},
        compiler_params=PARAMS,
        cost_estimate=cost(3 if pieces else 2, part, rows, d, SCALE[name]),
        name=name,
    )(scal, *u, *chunks, du, *extra)


def cycle_images(scal, u, caption, dv):
    rows, d = dv.shape
    return pl.pallas_call(
        images_kernel,
        grid=(rows // TILE,),
        in_specs=[SMEM, whole((rows, d)), blocks(TILE, d), blocks(TILE, d)],
        out_specs=blocks(TILE, d),
        out_shape=shape(rows, d),
        scratch_shapes=halves(rows, d),
        compiler_params=PARAMS,
        cost_estimate=cost(2, rows, rows, d),
        name="cyc_images",
    )(scal, u, caption, dv)


def returns(scal, u, captions, pieces, after):
    rows, d = u[0].shape
    part = captions.shape[0]
    tile = max(c for c in range(16, TILE + 128, 16) if part % c == 0)
    out = [(part, rows)] * 2 + [(part, d)] * 2
    return pl.pallas_call(
        functools.partial(returns_kernel, tile),
        grid=(part // tile,),
        in_specs=[SMEM] + [whole((rows, d))] * 2 + [blocks(tile, d), pl.BlockSpec(memory_space=pl.ANY)],
        out_specs=[blocks(tile, c) for _, c in out] + [result((n, d)) for n in pieces],
        out_shape=[shape(n, c, jnp.bfloat16) for n, c in out] + [shape(n, d) for n in pieces],
        compiler_params=PARAMS,
        cost_estimate=cost(2, part, rows, d, SCALE["part_b"]),
        name="part_b",
    )(scal, *u, captions, after)


def image_gradient(g, v, du, image):
    rows, d = du.shape
    part = v[0].shape[0]
    return pl.pallas_call(
        rest_kernel,
        grid=(rows // TILE,),
        in_specs=[pl.BlockSpec((part, TILE), lambda t: (0, t))] * 2 + [whole((part, d))] * 2 + [blocks(TILE, d)] * 2,
        out_specs=blocks(TILE, d),
        out_shape=shape(rows, d),
        compiler_params=PARAMS,
        cost_estimate=cost(1, part, rows, d, SCALE["rest"]),
        name="image_grad",
    )(*g, *v, du, image)


def finish(caption, base, part, at, grad=None):
    rows, d = caption.shape
    n = part.shape[0]
    tile = max(c for c in range(8, 200, 8) if n % c == 0 and at % c == 0)
    more = grad is not None
    return pl.pallas_call(
        finish_kernel,
        grid=(n // tile,),
        in_specs=[blocks(tile, d, at // tile)] * 2 + [blocks(tile, d)] + [pl.BlockSpec(memory_space=pl.ANY)] * more,
        out_specs=blocks(tile, d, at // tile),
        out_shape=shape(rows, d),
        input_output_aliases={3: 0} if more else {},
        compiler_params=SMALL,
        cost_estimate=pl.CostEstimate(flops=10 * part.size, bytes_accessed=16 * part.size, transcendentals=0),
        name="finish",
    )(caption, base, part, *([grad] if more else []))


def body(image_embed, caption_embed, pair_ids, log_scale, logit_bias):
    rows = image_embed.shape[0]
    chunks = [cut(caption_embed, a, b) for a, b in zip((0,) + CUTS, CUTS + (rows,))]
    parts = [partner(c, "grp") for c in chunks]
    cycles = [passed_along(c, "blk", 1) for c in chunks]
    scal = jnp.concatenate([jnp.exp(log_scale), logit_bias])
    first = (lax.axis_index("grp") * lax.axis_size("blk") + lax.axis_index("blk")) * rows
    one, hi, lo, du, dv = own_block(first.astype(jnp.int32)[None], scal, pair_ids[None, :], image_embed, caption_embed)
    u = (hi, lo)
    du, one, dv_part0 = score(scal, u, parts[:-1], du, [CUTS[-1]], "part_a", one)
    back0 = partner(dv_part0, "grp")
    next_u = passed_along(one, "blk", -1)
    (du,) = score(scal, u, cycles, du, [], "cyc_captions")
    edges = CUTS[-1:] + BACK + (rows,)
    pieces = [b - a for a, b in zip(edges, edges[1:])]
    g_hi, g_lo, v_hi, v_lo, *dv_part1 = returns(scal, u, parts[-1], pieces, du)
    backs = [partner(piece, "grp") for piece in dv_part1]
    base = cycle_images(scal, next_u, caption_embed, dv)
    image_grad = image_gradient((g_hi, g_lo), (v_hi, v_lo), du, image_embed)
    grad = finish(caption_embed, base, back0, 0)
    for at, back in zip(edges, backs):
        grad = finish(caption_embed, base, back, at, grad)
    return (image_grad, grad)


def solution(mesh):
    in_specs = (P(("grp", "blk"), None), P(("grp", "blk"), None), P(("grp", "blk")), P(), P())
    out_specs = (P(("grp", "blk"), None), P(("grp", "blk"), None))
    return jax.shard_map(body, mesh=mesh, in_specs=in_specs, out_specs=out_specs, check_vma=False)
```

```python
import functools

import jax
import jax.numpy as jnp
from jax import lax
from jax.experimental import pallas as pl
from jax.experimental.pallas import tpu as pltpu
from jax.sharding import PartitionSpec as P

EPS = 1e-06
TILE = 256
VMEM = 42
CUTS = (128, 384)
SCALE = dict(own=1.0, part_a=1.0, cyc_captions=1.0, part_b=3.0, rest=2.0)
BACK = (768, 960)
NT = (((1,), (1,)), ((), ()))
NN = (((1,), (0,)), ((), ()))
TN = (((0,), (0,)), ((), ()))
F32 = jnp.float32
SMEM = pl.BlockSpec(memory_space=pltpu.SMEM)
PARAMS = pltpu.CompilerParams(vmem_limit_bytes=VMEM * 1024 * 1024)
SMALL = pltpu.CompilerParams(vmem_limit_bytes=12 * 1024 * 1024)


def passed_along(block, axis, distance):
    n = lax.axis_size(axis)
    return lax.ppermute(block, axis, [((i - distance) % n, i) for i in range(n)])


def partner(block, axis):
    n = lax.axis_size(axis)
    return lax.ppermute(block, axis, [(i, (i + n // 2) % n) for i in range(n)])


def split(x):
    hi = x.astype(jnp.bfloat16)
    lo = (x - hi.astype(F32)).astype(jnp.bfloat16)
    return hi, lo


def product(a, b, dims):
    dot = functools.partial(lax.dot_general, dimension_numbers=dims, preferred_element_type=F32)
    return dot(a[0], b[0]) + (dot(a[0], b[1]) + dot(a[1], b[0]))


def norm_of(x):
    return jnp.sqrt(jnp.sum(x * x, axis=-1, keepdims=True) + EPS)


def unit(x):
    return x * (1.0 / norm_of(x))


def projected(raw, grad):
    r = 1.0 / norm_of(raw)
    one = raw * r
    return (grad - one * jnp.sum(one * grad, axis=-1, keepdims=True)) * r


def weights(u, v, scal_ref, labels=None):
    weight = jax.nn.sigmoid(scal_ref[0] * product(v, u, NT) + scal_ref[1])
    if labels is not None:
        weight = weight - labels
    return split(scal_ref[0] * weight)


def own_kernel(first_ref, scal_ref, ids_ref, image_ref, caption_ref, after_ref, u_ref, hi_ref, lo_ref, du_ref, dv_ref):
    del after_ref
    t = pl.program_id(0)
    tile = caption_ref.shape[0]

    @pl.when(t == 0)
    def _():
        u = unit(image_ref[...])
        u_ref[...] = u
        hi_ref[...], lo_ref[...] = split(u)
        du_ref[...] = jnp.zeros_like(du_ref)

    columns = first_ref[0] + t * tile + lax.broadcasted_iota(jnp.int32, (tile, ids_ref.shape[1]), 0)
    labels = (ids_ref[...] == columns).astype(F32)
    u = (hi_ref[...], lo_ref[...])
    v = split(unit(caption_ref[...]))
    g = weights(u, v, scal_ref, labels)
    dv_ref[...] = product(g, u, NN)
    du_ref[...] += product(g, v, TN)


def score_kernel(chunks, passed, tile, scal_ref, hi_ref, lo_ref, *rest):
    caption_refs, du_in_ref, du_ref = rest[:chunks], rest[chunks], rest[chunks + 1 + passed]
    dv_refs, (v_hi_ref, v_lo_ref) = rest[chunks + 2 + 2 * passed : -2], rest[-2:]
    t = pl.program_id(0)

    @pl.when(t == 0)
    def _():
        at = 0
        for ref in caption_refs:
            n = ref.shape[0]
            v_hi_ref[at : at + n, :], v_lo_ref[at : at + n, :] = split(unit(ref[...]))
            at += n
        du_ref[...] = du_in_ref[...]

    rows = pl.ds(pl.multiple_of(t * tile, 16), tile)
    u = (hi_ref[...], lo_ref[...])
    v = (v_hi_ref[rows, :], v_lo_ref[rows, :])
    g = weights(u, v, scal_ref)
    if dv_refs:
        dv = product(g, u, NN)
        for step in range(v_hi_ref.shape[0] // tile):

            @pl.when(t == step)
            def _():
                at = 0
                for ref in dv_refs:
                    a, b = max(at, step * tile), min(at + ref.shape[0], (step + 1) * tile)
                    if a < b:
                        ref[a - at : b - at, :] = dv[a - step * tile : b - step * tile, :]
                    at += ref.shape[0]

    du_ref[...] += product(g, v, TN)


def returns_kernel(tile, scal_ref, hi_ref, lo_ref, caption_ref, after_ref, g_hi_ref, g_lo_ref, v_hi_ref, v_lo_ref, *dv_refs):
    del after_ref
    t = pl.program_id(0)
    u = (hi_ref[...], lo_ref[...])
    v = split(unit(caption_ref[...]))
    v_hi_ref[...], v_lo_ref[...] = v
    g = weights(u, v, scal_ref)
    g_hi_ref[...], g_lo_ref[...] = g
    dv = product(g, u, NN)
    for step in range(sum(ref.shape[0] for ref in dv_refs) // tile):

        @pl.when(t == step)
        def _():
            at = 0
            for ref in dv_refs:
                a, b = max(at, step * tile), min(at + ref.shape[0], (step + 1) * tile)
                if a < b:
                    ref[a - at : b - at, :] = dv[a - step * tile : b - step * tile, :]
                at += ref.shape[0]


def rest_kernel(g_hi_ref, g_lo_ref, v_hi_ref, v_lo_ref, du_ref, image_ref, grad_ref):
    du = du_ref[...] + product((g_hi_ref[...], g_lo_ref[...]), (v_hi_ref[...], v_lo_ref[...]), TN)
    grad_ref[...] = projected(image_ref[...], du)


def images_kernel(scal_ref, u_ref, caption_ref, dv_in_ref, dv_ref, hi_ref, lo_ref):
    @pl.when(pl.program_id(0) == 0)
    def _():
        hi_ref[...], lo_ref[...] = split(u_ref[...])

    u = (hi_ref[...], lo_ref[...])
    g = weights(u, split(unit(caption_ref[...])), scal_ref)
    dv_ref[...] = dv_in_ref[...] + product(g, u, NN)


def finish_kernel(caption_ref, base_ref, part_ref, *rest):
    rest[-1][...] = projected(caption_ref[...], base_ref[...] + part_ref[...])


def whole(shape):
    return pl.BlockSpec(shape, lambda t: (0,) * len(shape), pipeline_mode=pl.Buffered(1))


def result(shape):
    return pl.BlockSpec(shape, lambda t: (0,) * len(shape))


def blocks(tile, d, first=0):
    return pl.BlockSpec((tile, d), lambda t: (t + first, 0))


def shape(rows, d, dtype=F32):
    return jax.ShapeDtypeStruct((rows, d), dtype)


def halves(rows, d):
    return [pltpu.VMEM((rows, d), jnp.bfloat16)] * 2


def cost(products, rows, cols, d, scale=1.0):
    return pl.CostEstimate(flops=int(scale * 2 * 3 * products * rows * cols * d), bytes_accessed=16 * rows * d, transcendentals=rows * cols)


def own_block(first, scal, ids, image, caption, after):
    rows, d = image.shape
    return pl.pallas_call(
        own_kernel,
        grid=(rows // TILE,),
        in_specs=[SMEM, SMEM, whole((1, rows)), whole((rows, d)), blocks(TILE, d), pl.BlockSpec(memory_space=pl.ANY)],
        out_specs=[result((rows, d))] * 4 + [blocks(TILE, d)],
        out_shape=[shape(rows, d)] + [shape(rows, d, jnp.bfloat16)] * 2 + [shape(rows, d)] * 2,
        compiler_params=PARAMS,
        cost_estimate=cost(3, rows, rows, d, SCALE['own']),
        name="own",
    )(first, scal, ids, image, caption, after)


def score(scal, u, chunks, du, pieces, name, passed=None):
    rows, d = du.shape
    part = sum(c.shape[0] for c in chunks)
    tile = max(c for c in range(16, TILE + 128, 16) if part % c == 0)
    extra = [] if passed is None else [passed]
    kept = [pl.BlockSpec(memory_space=pl.ANY)] * len(extra)
    return pl.pallas_call(
        functools.partial(score_kernel, len(chunks), len(extra), tile),
        grid=(part // tile,),
        in_specs=[SMEM] + [whole((rows, d))] * 2 + [whole(c.shape) for c in chunks] + [whole((rows, d))] + kept,
        out_specs=[result((rows, d))] + kept + [result((n, d)) for n in pieces],
        out_shape=[shape(rows, d)] + [shape(*x.shape) for x in extra] + [shape(n, d) for n in pieces],
        scratch_shapes=halves(part, d),
        input_output_aliases={4 + len(chunks): 1} if extra else {},
        compiler_params=PARAMS,
        cost_estimate=cost(3 if pieces else 2, part, rows, d, SCALE[name]),
        name=name,
    )(scal, *u, *chunks, du, *extra)


def cycle_images(scal, u, caption, dv):
    rows, d = dv.shape
    return pl.pallas_call(
        images_kernel,
        grid=(rows // TILE,),
        in_specs=[SMEM, whole((rows, d)), blocks(TILE, d), blocks(TILE, d)],
        out_specs=blocks(TILE, d),
        out_shape=shape(rows, d),
        scratch_shapes=halves(rows, d),
        compiler_params=PARAMS,
        cost_estimate=cost(2, rows, rows, d),
        name="cyc_images",
    )(scal, u, caption, dv)


def returns(scal, u, captions, pieces, after):
    rows, d = u[0].shape
    part = captions.shape[0]
    tile = max(c for c in range(16, TILE + 128, 16) if part % c == 0)
    out = [(part, rows)] * 2 + [(part, d)] * 2
    return pl.pallas_call(
        functools.partial(returns_kernel, tile),
        grid=(part // tile,),
        in_specs=[SMEM] + [whole((rows, d))] * 2 + [blocks(tile, d), pl.BlockSpec(memory_space=pl.ANY)],
        out_specs=[blocks(tile, c) for _, c in out] + [result((n, d)) for n in pieces],
        out_shape=[shape(n, c, jnp.bfloat16) for n, c in out] + [shape(n, d) for n in pieces],
        compiler_params=PARAMS,
        cost_estimate=cost(2, part, rows, d, SCALE["part_b"]),
        name="part_b",
    )(scal, *u, captions, after)


def image_gradient(g, v, du, image):
    rows, d = du.shape
    part = v[0].shape[0]
    return pl.pallas_call(
        rest_kernel,
        grid=(rows // TILE,),
        in_specs=[pl.BlockSpec((part, TILE), lambda t: (0, t))] * 2 + [whole((part, d))] * 2 + [blocks(TILE, d)] * 2,
        out_specs=blocks(TILE, d),
        out_shape=shape(rows, d),
        compiler_params=PARAMS,
        cost_estimate=cost(1, part, rows, d, SCALE["rest"]),
        name="image_grad",
    )(*g, *v, du, image)


def finish(caption, base, part, at, grad=None):
    rows, d = caption.shape
    n = part.shape[0]
    tile = max(c for c in range(8, 200, 8) if n % c == 0 and at % c == 0)
    more = grad is not None
    return pl.pallas_call(
        finish_kernel,
        grid=(n // tile,),
        in_specs=[blocks(tile, d, at // tile)] * 2 + [blocks(tile, d)] + [pl.BlockSpec(memory_space=pl.ANY)] * more,
        out_specs=blocks(tile, d, at // tile),
        out_shape=shape(rows, d),
        input_output_aliases={3: 0} if more else {},
        compiler_params=SMALL,
        cost_estimate=pl.CostEstimate(flops=10 * part.size, bytes_accessed=16 * part.size, transcendentals=0),
        name="finish",
    )(caption, base, part, *([grad] if more else []))


def body(image_embed, caption_embed, pair_ids, log_scale, logit_bias):
    rows = image_embed.shape[0]
    chunks, later = [], caption_embed
    for a, b in zip((0,) + CUTS, CUTS + (rows,)):
        chunk, later = lax.optimization_barrier((later[a:b], later))
        chunks.append(chunk)
    parts = [partner(c, "grp") for c in chunks]
    cycles = [passed_along(c, "blk", 1) for c in chunks]
    scal = jnp.concatenate([jnp.exp(log_scale), logit_bias])
    first = (lax.axis_index("grp") * lax.axis_size("blk") + lax.axis_index("blk")) * rows
    one, hi, lo, du, dv = own_block(first.astype(jnp.int32)[None], scal, pair_ids[None, :], image_embed, caption_embed, parts[0])
    u = (hi, lo)
    du, one, dv_part0 = score(scal, u, parts[:-1], du, [CUTS[-1]], "part_a", one)
    back0 = partner(dv_part0, "grp")
    next_u = passed_along(one, "blk", -1)
    (du,) = score(scal, u, cycles, du, [], "cyc_captions")
    edges = CUTS[-1:] + BACK + (rows,)
    pieces = [b - a for a, b in zip(edges, edges[1:])]
    g_hi, g_lo, v_hi, v_lo, *dv_part1 = returns(scal, u, parts[-1], pieces, du)
    backs = [partner(piece, "grp") for piece in dv_part1]
    base = cycle_images(scal, next_u, caption_embed, dv)
    image_grad = image_gradient((g_hi, g_lo), (v_hi, v_lo), du, image_embed)
    grad = finish(caption_embed, base, back0, 0)
    for at, back in zip(edges, backs):
        grad = finish(caption_embed, base, back, at, grad)
    return (image_grad, grad)


def solution(mesh):
    in_specs = (P(("grp", "blk"), None), P(("grp", "blk"), None), P(("grp", "blk")), P(), P())
    out_specs = (P(("grp", "blk"), None), P(("grp", "blk"), None))
    return jax.shard_map(body, mesh=mesh, in_specs=in_specs, out_specs=out_specs, check_vma=False)
```

```python
import functools

import jax
import jax.numpy as jnp
from jax import lax
from jax.experimental import pallas as pl
from jax.experimental.pallas import tpu as pltpu
from jax.sharding import PartitionSpec as P

EPS = 1e-06
TILE = 256
VMEM = 50
CUTS = (128, 384)
SCALE = dict(own=1.0, part_a=1.0, cyc_captions=1.0, part_b=3.0, rest=2.0)
BACK = (768, 960)
NT = (((1,), (1,)), ((), ()))
NN = (((1,), (0,)), ((), ()))
TN = (((0,), (0,)), ((), ()))
F32 = jnp.float32
SMEM = pl.BlockSpec(memory_space=pltpu.SMEM)
PARAMS = pltpu.CompilerParams(vmem_limit_bytes=VMEM * 1024 * 1024)
SMALL = pltpu.CompilerParams(vmem_limit_bytes=12 * 1024 * 1024)


def passed_along(block, axis, distance):
    n = lax.axis_size(axis)
    return lax.ppermute(block, axis, [((i - distance) % n, i) for i in range(n)])


def partner(block, axis):
    n = lax.axis_size(axis)
    return lax.ppermute(block, axis, [(i, (i + n // 2) % n) for i in range(n)])


def split(x):
    hi = x.astype(jnp.bfloat16)
    lo = (x - hi.astype(F32)).astype(jnp.bfloat16)
    return hi, lo


def product(a, b, dims):
    dot = functools.partial(lax.dot_general, dimension_numbers=dims, preferred_element_type=F32)
    return dot(a[0], b[0]) + (dot(a[0], b[1]) + dot(a[1], b[0]))


def norm_of(x):
    return jnp.sqrt(jnp.sum(x * x, axis=-1, keepdims=True) + EPS)


def unit(x):
    return x * (1.0 / norm_of(x))


def projected(raw, grad):
    r = 1.0 / norm_of(raw)
    one = raw * r
    return (grad - one * jnp.sum(one * grad, axis=-1, keepdims=True)) * r


def weights(u, v, scal_ref, labels=None):
    weight = jax.nn.sigmoid(scal_ref[0] * product(v, u, NT) + scal_ref[1])
    if labels is not None:
        weight = weight - labels
    return split(scal_ref[0] * weight)


def own_kernel(first_ref, scal_ref, ids_ref, image_ref, caption_ref, after_ref, u_ref, hi_ref, lo_ref, du_ref, dv_ref):
    del after_ref
    t = pl.program_id(0)
    tile = caption_ref.shape[0]

    @pl.when(t == 0)
    def _():
        u = unit(image_ref[...])
        u_ref[...] = u
        hi_ref[...], lo_ref[...] = split(u)
        du_ref[...] = jnp.zeros_like(du_ref)

    columns = first_ref[0] + t * tile + lax.broadcasted_iota(jnp.int32, (tile, ids_ref.shape[1]), 0)
    labels = (ids_ref[...] == columns).astype(F32)
    u = (hi_ref[...], lo_ref[...])
    v = split(unit(caption_ref[...]))
    g = weights(u, v, scal_ref, labels)
    dv_ref[...] = product(g, u, NN)
    du_ref[...] += product(g, v, TN)


def score_kernel(chunks, passed, tile, scal_ref, hi_ref, lo_ref, *rest):
    caption_refs, du_in_ref, du_ref = rest[:chunks], rest[chunks], rest[chunks + 1 + passed]
    dv_refs, (v_hi_ref, v_lo_ref) = rest[chunks + 2 + 2 * passed : -2], rest[-2:]
    t = pl.program_id(0)

    @pl.when(t == 0)
    def _():
        at = 0
        for ref in caption_refs:
            n = ref.shape[0]
            v_hi_ref[at : at + n, :], v_lo_ref[at : at + n, :] = split(unit(ref[...]))
            at += n
        du_ref[...] = du_in_ref[...]

    rows = pl.ds(pl.multiple_of(t * tile, 16), tile)
    u = (hi_ref[...], lo_ref[...])
    v = (v_hi_ref[rows, :], v_lo_ref[rows, :])
    g = weights(u, v, scal_ref)
    if dv_refs:
        dv = product(g, u, NN)
        for step in range(v_hi_ref.shape[0] // tile):

            @pl.when(t == step)
            def _():
                at = 0
                for ref in dv_refs:
                    a, b = max(at, step * tile), min(at + ref.shape[0], (step + 1) * tile)
                    if a < b:
                        ref[a - at : b - at, :] = dv[a - step * tile : b - step * tile, :]
                    at += ref.shape[0]

    du_ref[...] += product(g, v, TN)


def returns_kernel(tile, scal_ref, hi_ref, lo_ref, caption_ref, after_ref, g_hi_ref, g_lo_ref, v_hi_ref, v_lo_ref, *dv_refs):
    del after_ref
    t = pl.program_id(0)
    u = (hi_ref[...], lo_ref[...])
    v = split(unit(caption_ref[...]))
    v_hi_ref[...], v_lo_ref[...] = v
    g = weights(u, v, scal_ref)
    g_hi_ref[...], g_lo_ref[...] = g
    dv = product(g, u, NN)
    for step in range(sum(ref.shape[0] for ref in dv_refs) // tile):

        @pl.when(t == step)
        def _():
            at = 0
            for ref in dv_refs:
                a, b = max(at, step * tile), min(at + ref.shape[0], (step + 1) * tile)
                if a < b:
                    ref[a - at : b - at, :] = dv[a - step * tile : b - step * tile, :]
                at += ref.shape[0]


def rest_kernel(g_hi_ref, g_lo_ref, v_hi_ref, v_lo_ref, du_ref, image_ref, grad_ref):
    du = du_ref[...] + product((g_hi_ref[...], g_lo_ref[...]), (v_hi_ref[...], v_lo_ref[...]), TN)
    grad_ref[...] = projected(image_ref[...], du)


def images_kernel(scal_ref, u_ref, caption_ref, dv_in_ref, dv_ref, hi_ref, lo_ref):
    @pl.when(pl.program_id(0) == 0)
    def _():
        hi_ref[...], lo_ref[...] = split(u_ref[...])

    u = (hi_ref[...], lo_ref[...])
    g = weights(u, split(unit(caption_ref[...])), scal_ref)
    dv_ref[...] = dv_in_ref[...] + product(g, u, NN)


def finish_kernel(caption_ref, base_ref, part_ref, *rest):
    rest[-1][...] = projected(caption_ref[...], base_ref[...] + part_ref[...])


def whole(shape):
    return pl.BlockSpec(shape, lambda t: (0,) * len(shape), pipeline_mode=pl.Buffered(1))


def result(shape):
    return pl.BlockSpec(shape, lambda t: (0,) * len(shape))


def blocks(tile, d, first=0):
    return pl.BlockSpec((tile, d), lambda t: (t + first, 0))


def shape(rows, d, dtype=F32):
    return jax.ShapeDtypeStruct((rows, d), dtype)


def halves(rows, d):
    return [pltpu.VMEM((rows, d), jnp.bfloat16)] * 2


def cost(products, rows, cols, d, scale=1.0):
    return pl.CostEstimate(flops=int(scale * 2 * 3 * products * rows * cols * d), bytes_accessed=16 * rows * d, transcendentals=rows * cols)


def own_block(first, scal, ids, image, caption, after):
    rows, d = image.shape
    return pl.pallas_call(
        own_kernel,
        grid=(rows // TILE,),
        in_specs=[SMEM, SMEM, whole((1, rows)), whole((rows, d)), blocks(TILE, d), pl.BlockSpec(memory_space=pl.ANY)],
        out_specs=[result((rows, d))] * 4 + [blocks(TILE, d)],
        out_shape=[shape(rows, d)] + [shape(rows, d, jnp.bfloat16)] * 2 + [shape(rows, d)] * 2,
        compiler_params=PARAMS,
        cost_estimate=cost(3, rows, rows, d, SCALE['own']),
        name="own",
    )(first, scal, ids, image, caption, after)


def score(scal, u, chunks, du, pieces, name, passed=None):
    rows, d = du.shape
    part = sum(c.shape[0] for c in chunks)
    tile = max(c for c in range(16, TILE + 128, 16) if part % c == 0)
    extra = [] if passed is None else [passed]
    kept = [pl.BlockSpec(memory_space=pl.ANY)] * len(extra)
    return pl.pallas_call(
        functools.partial(score_kernel, len(chunks), len(extra), tile),
        grid=(part // tile,),
        in_specs=[SMEM] + [whole((rows, d))] * 2 + [whole(c.shape) for c in chunks] + [whole((rows, d))] + kept,
        out_specs=[result((rows, d))] + kept + [result((n, d)) for n in pieces],
        out_shape=[shape(rows, d)] + [shape(*x.shape) for x in extra] + [shape(n, d) for n in pieces],
        scratch_shapes=halves(part, d),
        input_output_aliases={4 + len(chunks): 1} if extra else {},
        compiler_params=PARAMS,
        cost_estimate=cost(3 if pieces else 2, part, rows, d, SCALE[name]),
        name=name,
    )(scal, *u, *chunks, du, *extra)


def cycle_images(scal, u, caption, dv):
    rows, d = dv.shape
    return pl.pallas_call(
        images_kernel,
        grid=(rows // TILE,),
        in_specs=[SMEM, whole((rows, d)), blocks(TILE, d), blocks(TILE, d)],
        out_specs=blocks(TILE, d),
        out_shape=shape(rows, d),
        scratch_shapes=halves(rows, d),
        compiler_params=PARAMS,
        cost_estimate=cost(2, rows, rows, d),
        name="cyc_images",
    )(scal, u, caption, dv)


def returns(scal, u, captions, pieces, after):
    rows, d = u[0].shape
    part = captions.shape[0]
    tile = max(c for c in range(16, TILE + 128, 16) if part % c == 0)
    out = [(part, rows)] * 2 + [(part, d)] * 2
    return pl.pallas_call(
        functools.partial(returns_kernel, tile),
        grid=(part // tile,),
        in_specs=[SMEM] + [whole((rows, d))] * 2 + [blocks(tile, d), pl.BlockSpec(memory_space=pl.ANY)],
        out_specs=[blocks(tile, c) for _, c in out] + [result((n, d)) for n in pieces],
        out_shape=[shape(n, c, jnp.bfloat16) for n, c in out] + [shape(n, d) for n in pieces],
        compiler_params=PARAMS,
        cost_estimate=cost(2, part, rows, d, SCALE["part_b"]),
        name="part_b",
    )(scal, *u, captions, after)


def image_gradient(g, v, du, image):
    rows, d = du.shape
    part = v[0].shape[0]
    return pl.pallas_call(
        rest_kernel,
        grid=(rows // TILE,),
        in_specs=[pl.BlockSpec((part, TILE), lambda t: (0, t))] * 2 + [whole((part, d))] * 2 + [blocks(TILE, d)] * 2,
        out_specs=blocks(TILE, d),
        out_shape=shape(rows, d),
        compiler_params=PARAMS,
        cost_estimate=cost(1, part, rows, d, SCALE["rest"]),
        name="image_grad",
    )(*g, *v, du, image)


def finish(caption, base, part, at, grad=None):
    rows, d = caption.shape
    n = part.shape[0]
    tile = max(c for c in range(8, 200, 8) if n % c == 0 and at % c == 0)
    more = grad is not None
    return pl.pallas_call(
        finish_kernel,
        grid=(n // tile,),
        in_specs=[blocks(tile, d, at // tile)] * 2 + [blocks(tile, d)] + [pl.BlockSpec(memory_space=pl.ANY)] * more,
        out_specs=blocks(tile, d, at // tile),
        out_shape=shape(rows, d),
        input_output_aliases={3: 0} if more else {},
        compiler_params=SMALL,
        cost_estimate=pl.CostEstimate(flops=10 * part.size, bytes_accessed=16 * part.size, transcendentals=0),
        name="finish",
    )(caption, base, part, *([grad] if more else []))


def body(image_embed, caption_embed, pair_ids, log_scale, logit_bias):
    rows = image_embed.shape[0]
    chunks, later = [], caption_embed
    for a, b in zip((0,) + CUTS, CUTS + (rows,)):
        chunk, later = lax.optimization_barrier((later[a:b], later))
        chunks.append(chunk)
    parts = [partner(c, "grp") for c in chunks]
    cycles = [passed_along(c, "blk", 1) for c in chunks]
    scal = jnp.concatenate([jnp.exp(log_scale), logit_bias])
    first = (lax.axis_index("grp") * lax.axis_size("blk") + lax.axis_index("blk")) * rows
    one, hi, lo, du, dv = own_block(first.astype(jnp.int32)[None], scal, pair_ids[None, :], image_embed, caption_embed, parts[0])
    u = (hi, lo)
    du, one, dv_part0 = score(scal, u, parts[:-1], du, [CUTS[-1]], "part_a", one)
    back0 = partner(dv_part0, "grp")
    next_u = passed_along(one, "blk", -1)
    (du,) = score(scal, u, cycles, du, [], "cyc_captions")
    edges = CUTS[-1:] + BACK + (rows,)
    pieces = [b - a for a, b in zip(edges, edges[1:])]
    g_hi, g_lo, v_hi, v_lo, *dv_part1 = returns(scal, u, parts[-1], pieces, du)
    backs = [partner(piece, "grp") for piece in dv_part1]
    base = cycle_images(scal, next_u, caption_embed, dv)
    image_grad = image_gradient((g_hi, g_lo), (v_hi, v_lo), du, image_embed)
    grad = finish(caption_embed, base, back0, 0)
    for at, back in zip(edges, backs):
        grad = finish(caption_embed, base, back, at, grad)
    return (image_grad, grad)


def solution(mesh):
    in_specs = (P(("grp", "blk"), None), P(("grp", "blk"), None), P(("grp", "blk")), P(), P())
    out_specs = (P(("grp", "blk"), None), P(("grp", "blk"), None))
    return jax.shard_map(body, mesh=mesh, in_specs=in_specs, out_specs=out_specs, check_vma=False)
```

```python
import functools

import jax
import jax.numpy as jnp
from jax import lax
from jax.experimental import pallas as pl
from jax.experimental.pallas import tpu as pltpu
from jax.sharding import PartitionSpec as P

EPS = 1e-06
TILE = 256
VMEM = 48
CUTS = (128, 512)
SCALE = dict(own=1.0, part_a=1.0, cyc_captions=1.0, part_b=3.0, rest=2.0)
BACK = (768, 960)
NT = (((1,), (1,)), ((), ()))
NN = (((1,), (0,)), ((), ()))
TN = (((0,), (0,)), ((), ()))
F32 = jnp.float32
SMEM = pl.BlockSpec(memory_space=pltpu.SMEM)
PARAMS = pltpu.CompilerParams(vmem_limit_bytes=VMEM * 1024 * 1024)
SMALL = pltpu.CompilerParams(vmem_limit_bytes=12 * 1024 * 1024)


def passed_along(block, axis, distance):
    n = lax.axis_size(axis)
    return lax.ppermute(block, axis, [((i - distance) % n, i) for i in range(n)])


def partner(block, axis):
    n = lax.axis_size(axis)
    return lax.ppermute(block, axis, [(i, (i + n // 2) % n) for i in range(n)])


def towards_partner(block):
    n, m = lax.axis_size("grp"), lax.axis_size("blk")
    step = n // 4
    route = [(g * m + k, (g + (-step if k % 2 else step)) % n * m + k) for g in range(n) for k in range(m)]
    return lax.ppermute(block, ("grp", "blk"), route)


def split(x):
    hi = x.astype(jnp.bfloat16)
    lo = (x - hi.astype(F32)).astype(jnp.bfloat16)
    return hi, lo


def product(a, b, dims):
    dot = functools.partial(lax.dot_general, dimension_numbers=dims, preferred_element_type=F32)
    return dot(a[0], b[0]) + (dot(a[0], b[1]) + dot(a[1], b[0]))


def norm_of(x):
    return jnp.sqrt(jnp.sum(x * x, axis=-1, keepdims=True) + EPS)


def unit(x):
    return x * (1.0 / norm_of(x))


def projected(raw, grad):
    r = 1.0 / norm_of(raw)
    one = raw * r
    return (grad - one * jnp.sum(one * grad, axis=-1, keepdims=True)) * r


def weights(u, v, scal_ref, labels=None):
    weight = jax.nn.sigmoid(scal_ref[0] * product(v, u, NT) + scal_ref[1])
    if labels is not None:
        weight = weight - labels
    return split(scal_ref[0] * weight)


def own_kernel(first_ref, scal_ref, ids_ref, image_ref, caption_ref, after_ref, u_ref, hi_ref, lo_ref, du_ref, dv_ref):
    del after_ref
    t = pl.program_id(0)
    tile = caption_ref.shape[0]

    @pl.when(t == 0)
    def _():
        u = unit(image_ref[...])
        u_ref[...] = u
        hi_ref[...], lo_ref[...] = split(u)
        du_ref[...] = jnp.zeros_like(du_ref)

    columns = first_ref[0] + t * tile + lax.broadcasted_iota(jnp.int32, (tile, ids_ref.shape[1]), 0)
    labels = (ids_ref[...] == columns).astype(F32)
    u = (hi_ref[...], lo_ref[...])
    v = split(unit(caption_ref[...]))
    g = weights(u, v, scal_ref, labels)
    dv_ref[...] = product(g, u, NN)
    du_ref[...] += product(g, v, TN)


def score_kernel(chunks, passed, tile, scal_ref, hi_ref, lo_ref, *rest):
    caption_refs, du_in_ref, du_ref = rest[:chunks], rest[chunks], rest[chunks + 1 + passed]
    dv_refs, (v_hi_ref, v_lo_ref) = rest[chunks + 2 + 2 * passed : -2], rest[-2:]
    t = pl.program_id(0)

    @pl.when(t == 0)
    def _():
        at = 0
        for ref in caption_refs:
            n = ref.shape[0]
            v_hi_ref[at : at + n, :], v_lo_ref[at : at + n, :] = split(unit(ref[...]))
            at += n
        du_ref[...] = du_in_ref[...]

    rows = pl.ds(pl.multiple_of(t * tile, 16), tile)
    u = (hi_ref[...], lo_ref[...])
    v = (v_hi_ref[rows, :], v_lo_ref[rows, :])
    g = weights(u, v, scal_ref)
    if dv_refs:
        dv = product(g, u, NN)
        for step in range(v_hi_ref.shape[0] // tile):

            @pl.when(t == step)
            def _():
                at = 0
                for ref in dv_refs:
                    a, b = max(at, step * tile), min(at + ref.shape[0], (step + 1) * tile)
                    if a < b:
                        ref[a - at : b - at, :] = dv[a - step * tile : b - step * tile, :]
                    at += ref.shape[0]

    du_ref[...] += product(g, v, TN)


def returns_kernel(chunks, tile, scal_ref, hi_ref, lo_ref, *rest):
    caption_refs, (g_hi_ref, g_lo_ref, v_hi_ref, v_lo_ref), dv_refs = rest[:chunks], rest[chunks + 1 : chunks + 5], rest[chunks + 5 :]
    t = pl.program_id(0)

    @pl.when(t == 0)
    def _():
        at = 0
        for ref in caption_refs:
            n = ref.shape[0]
            v_hi_ref[at : at + n, :], v_lo_ref[at : at + n, :] = split(unit(ref[...]))
            at += n

    rows = pl.ds(pl.multiple_of(t * tile, 16), tile)
    u = (hi_ref[...], lo_ref[...])
    g = weights(u, (v_hi_ref[rows, :], v_lo_ref[rows, :]), scal_ref)
    g_hi_ref[...], g_lo_ref[...] = g
    dv = product(g, u, NN)
    for step in range(v_hi_ref.shape[0] // tile):

        @pl.when(t == step)
        def _():
            at = 0
            for ref in dv_refs:
                a, b = max(at, step * tile), min(at + ref.shape[0], (step + 1) * tile)
                if a < b:
                    ref[a - at : b - at, :] = dv[a - step * tile : b - step * tile, :]
                at += ref.shape[0]


def rest_kernel(g_hi_ref, g_lo_ref, v_hi_ref, v_lo_ref, du_ref, image_ref, grad_ref):
    du = du_ref[...] + product((g_hi_ref[...], g_lo_ref[...]), (v_hi_ref[...], v_lo_ref[...]), TN)
    grad_ref[...] = projected(image_ref[...], du)


def images_kernel(scal_ref, u_ref, caption_ref, dv_in_ref, dv_ref, hi_ref, lo_ref):
    @pl.when(pl.program_id(0) == 0)
    def _():
        hi_ref[...], lo_ref[...] = split(u_ref[...])

    u = (hi_ref[...], lo_ref[...])
    g = weights(u, split(unit(caption_ref[...])), scal_ref)
    dv_ref[...] = dv_in_ref[...] + product(g, u, NN)


def finish_kernel(caption_ref, base_ref, part_ref, *rest):
    rest[-1][...] = projected(caption_ref[...], base_ref[...] + part_ref[...])


def whole(shape):
    return pl.BlockSpec(shape, lambda t: (0,) * len(shape), pipeline_mode=pl.Buffered(1))


def result(shape):
    return pl.BlockSpec(shape, lambda t: (0,) * len(shape))


def blocks(tile, d, first=0):
    return pl.BlockSpec((tile, d), lambda t: (t + first, 0))


def shape(rows, d, dtype=F32):
    return jax.ShapeDtypeStruct((rows, d), dtype)


def halves(rows, d):
    return [pltpu.VMEM((rows, d), jnp.bfloat16)] * 2


def cost(products, rows, cols, d, scale=1.0):
    return pl.CostEstimate(flops=int(scale * 2 * 3 * products * rows * cols * d), bytes_accessed=16 * rows * d, transcendentals=rows * cols)


def own_block(first, scal, ids, image, caption, after):
    rows, d = image.shape
    return pl.pallas_call(
        own_kernel,
        grid=(rows // TILE,),
        in_specs=[SMEM, SMEM, whole((1, rows)), whole((rows, d)), blocks(TILE, d), pl.BlockSpec(memory_space=pl.ANY)],
        out_specs=[result((rows, d))] * 4 + [blocks(TILE, d)],
        out_shape=[shape(rows, d)] + [shape(rows, d, jnp.bfloat16)] * 2 + [shape(rows, d)] * 2,
        compiler_params=PARAMS,
        cost_estimate=cost(3, rows, rows, d, SCALE['own']),
        name="own",
    )(first, scal, ids, image, caption, after)


def score(scal, u, chunks, du, pieces, name, passed=None):
    rows, d = du.shape
    part = sum(c.shape[0] for c in chunks)
    tile = max(c for c in range(16, TILE + 128, 16) if part % c == 0)
    extra = [] if passed is None else [passed]
    kept = [pl.BlockSpec(memory_space=pl.ANY)] * len(extra)
    return pl.pallas_call(
        functools.partial(score_kernel, len(chunks), len(extra), tile),
        grid=(part // tile,),
        in_specs=[SMEM] + [whole((rows, d))] * 2 + [whole(c.shape) for c in chunks] + [whole((rows, d))] + kept,
        out_specs=[result((rows, d))] + kept + [result((n, d)) for n in pieces],
        out_shape=[shape(rows, d)] + [shape(*x.shape) for x in extra] + [shape(n, d) for n in pieces],
        scratch_shapes=halves(part, d),
        input_output_aliases={4 + len(chunks): 1} if extra else {},
        compiler_params=PARAMS,
        cost_estimate=cost(3 if pieces else 2, part, rows, d, SCALE[name]),
        name=name,
    )(scal, *u, *chunks, du, *extra)


def cycle_images(scal, u, caption, dv):
    rows, d = dv.shape
    return pl.pallas_call(
        images_kernel,
        grid=(rows // TILE,),
        in_specs=[SMEM, whole((rows, d)), blocks(TILE, d), blocks(TILE, d)],
        out_specs=blocks(TILE, d),
        out_shape=shape(rows, d),
        scratch_shapes=halves(rows, d),
        compiler_params=PARAMS,
        cost_estimate=cost(2, rows, rows, d),
        name="cyc_images",
    )(scal, u, caption, dv)


def returns(scal, u, chunks, pieces, after):
    rows, d = u[0].shape
    part = sum(c.shape[0] for c in chunks)
    tile = max(c for c in range(16, TILE + 128, 16) if part % c == 0)
    return pl.pallas_call(
        functools.partial(returns_kernel, len(chunks), tile),
        grid=(part // tile,),
        in_specs=[SMEM] + [whole((rows, d))] * 2 + [whole(c.shape) for c in chunks] + [pl.BlockSpec(memory_space=pl.ANY)],
        out_specs=[blocks(tile, rows)] * 2 + [result((part, d))] * 2 + [result((n, d)) for n in pieces],
        out_shape=[shape(part, c, jnp.bfloat16) for c in (rows, rows, d, d)] + [shape(n, d) for n in pieces],
        compiler_params=PARAMS,
        cost_estimate=cost(2, part, rows, d, SCALE["part_b"]),
        name="part_b",
    )(scal, *u, *chunks, after)


def image_gradient(g, v, du, image):
    rows, d = du.shape
    part = v[0].shape[0]
    return pl.pallas_call(
        rest_kernel,
        grid=(rows // TILE,),
        in_specs=[pl.BlockSpec((part, TILE), lambda t: (0, t))] * 2 + [whole((part, d))] * 2 + [blocks(TILE, d)] * 2,
        out_specs=blocks(TILE, d),
        out_shape=shape(rows, d),
        compiler_params=PARAMS,
        cost_estimate=cost(1, part, rows, d, SCALE["rest"]),
        name="image_grad",
    )(*g, *v, du, image)


def finish(caption, base, part, at, grad=None):
    rows, d = caption.shape
    n = part.shape[0]
    tile = max(c for c in range(8, 200, 8) if n % c == 0 and at % c == 0)
    more = grad is not None
    return pl.pallas_call(
        finish_kernel,
        grid=(n // tile,),
        in_specs=[blocks(tile, d, at // tile)] * 2 + [blocks(tile, d)] + [pl.BlockSpec(memory_space=pl.ANY)] * more,
        out_specs=blocks(tile, d, at // tile),
        out_shape=shape(rows, d),
        input_output_aliases={3: 0} if more else {},
        compiler_params=SMALL,
        cost_estimate=pl.CostEstimate(flops=10 * part.size, bytes_accessed=16 * part.size, transcendentals=0),
        name="finish",
    )(caption, base, part, *([grad] if more else []))


def body(image_embed, caption_embed, pair_ids, log_scale, logit_bias):
    rows = image_embed.shape[0]
    chunks, later = [], caption_embed
    for a, b in zip((0,) + CUTS, CUTS + (rows,)):
        chunk, later = lax.optimization_barrier((later[a:b], later))
        chunks.append(chunk)
    near = towards_partner(chunks[0])
    parts = [towards_partner(near)] + [partner(c, "grp") for c in chunks[1:]]
    cycles = [passed_along(c, "blk", 1) for c in chunks]
    scal = jnp.concatenate([jnp.exp(log_scale), logit_bias])
    first = (lax.axis_index("grp") * lax.axis_size("blk") + lax.axis_index("blk")) * rows
    one, hi, lo, du, dv = own_block(first.astype(jnp.int32)[None], scal, pair_ids[None, :], image_embed, caption_embed, near)
    u = (hi, lo)
    head, middle = CUTS
    du, one, dv_part0 = score(scal, u, parts[1:2], du, [middle - head], "part_a", one)
    back0 = partner(dv_part0, "grp")
    next_u = passed_along(one, "blk", -1)
    (du,) = score(scal, u, cycles, du, [], "cyc_captions")
    edges = CUTS[-1:] + BACK + (rows,)
    pieces = [(0, head)] + [(a, b - a) for a, b in zip(edges, edges[1:])]
    g_hi, g_lo, v_hi, v_lo, *dv_part1 = returns(scal, u, [parts[0], parts[2]], [n for _, n in pieces], du)
    backs = [(n, at, partner(piece, "grp")) for (at, n), piece in zip(pieces, dv_part1)]
    base = cycle_images(scal, next_u, caption_embed, dv)
    image_grad = image_gradient((g_hi, g_lo), (v_hi, v_lo), du, image_embed)
    grad = finish(caption_embed, base, back0, head)
    for _, at, back in sorted(backs, key=lambda x: -x[0]):
        grad = finish(caption_embed, base, back, at, grad)
    return (image_grad, grad)


def solution(mesh):
    in_specs = (P(("grp", "blk"), None), P(("grp", "blk"), None), P(("grp", "blk")), P(), P())
    out_specs = (P(("grp", "blk"), None), P(("grp", "blk"), None))
    return jax.shard_map(body, mesh=mesh, in_specs=in_specs, out_specs=out_specs, check_vma=False)
```

```python
import functools

import jax
import jax.numpy as jnp
from jax import lax
from jax.experimental import pallas as pl
from jax.experimental.pallas import tpu as pltpu
from jax.sharding import PartitionSpec as P

EPS = 1e-06
TILE = 256
VMEM = 50
CUTS = (128, 384)
SCALE = dict(own=1.0, part_a=1.0, cyc_captions=1.0, part_b=3.0, rest=2.0)
BACK = (768, 960)
NT = (((1,), (1,)), ((), ()))
NN = (((1,), (0,)), ((), ()))
TN = (((0,), (0,)), ((), ()))
F32 = jnp.float32
SMEM = pl.BlockSpec(memory_space=pltpu.SMEM)
PARAMS = pltpu.CompilerParams(vmem_limit_bytes=VMEM * 1024 * 1024)
SMALL = pltpu.CompilerParams(vmem_limit_bytes=12 * 1024 * 1024)


def passed_along(block, axis, distance):
    n = lax.axis_size(axis)
    return lax.ppermute(block, axis, [((i - distance) % n, i) for i in range(n)])


def partner(block, axis):
    n = lax.axis_size(axis)
    return lax.ppermute(block, axis, [(i, (i + n // 2) % n) for i in range(n)])


def split(x):
    hi = x.astype(jnp.bfloat16)
    lo = (x - hi.astype(F32)).astype(jnp.bfloat16)
    return hi, lo


def product(a, b, dims):
    dot = functools.partial(lax.dot_general, dimension_numbers=dims, preferred_element_type=F32)
    return dot(a[0], b[0]) + (dot(a[0], b[1]) + dot(a[1], b[0]))


def norm_of(x):
    return jnp.sqrt(jnp.sum(x * x, axis=-1, keepdims=True) + EPS)


def unit(x):
    return x * (1.0 / norm_of(x))


def projected(raw, grad):
    r = 1.0 / norm_of(raw)
    one = raw * r
    return (grad - one * jnp.sum(one * grad, axis=-1, keepdims=True)) * r


def weights(u, v, scal_ref, labels=None):
    weight = jax.nn.sigmoid(scal_ref[0] * product(v, u, NT) + scal_ref[1])
    if labels is not None:
        weight = weight - labels
    return split(scal_ref[0] * weight)


def own_kernel(first_ref, scal_ref, ids_ref, image_ref, caption_ref, after_ref, u_ref, hi_ref, lo_ref, du_ref, dv_ref):
    del after_ref
    t = pl.program_id(0)
    tile = caption_ref.shape[0]

    @pl.when(t == 0)
    def _():
        u = unit(image_ref[...])
        u_ref[...] = u
        hi_ref[...], lo_ref[...] = split(u)
        du_ref[...] = jnp.zeros_like(du_ref)

    columns = first_ref[0] + t * tile + lax.broadcasted_iota(jnp.int32, (tile, ids_ref.shape[1]), 0)
    labels = (ids_ref[...] == columns).astype(F32)
    u = (hi_ref[...], lo_ref[...])
    v = split(unit(caption_ref[...]))
    g = weights(u, v, scal_ref, labels)
    dv_ref[...] = product(g, u, NN)
    du_ref[...] += product(g, v, TN)


def score_kernel(chunks, passed, tile, scal_ref, hi_ref, lo_ref, *rest):
    caption_refs, du_in_ref, du_ref = rest[:chunks], rest[chunks], rest[chunks + 1 + passed]
    dv_refs, (v_hi_ref, v_lo_ref) = rest[chunks + 2 + 2 * passed : -2], rest[-2:]
    t = pl.program_id(0)

    @pl.when(t == 0)
    def _():
        at = 0
        for ref in caption_refs:
            n = ref.shape[0]
            v_hi_ref[at : at + n, :], v_lo_ref[at : at + n, :] = split(unit(ref[...]))
            at += n
        du_ref[...] = du_in_ref[...]

    rows = pl.ds(pl.multiple_of(t * tile, 16), tile)
    u = (hi_ref[...], lo_ref[...])
    v = (v_hi_ref[rows, :], v_lo_ref[rows, :])
    g = weights(u, v, scal_ref)
    if dv_refs:
        dv = product(g, u, NN)
        for step in range(v_hi_ref.shape[0] // tile):

            @pl.when(t == step)
            def _():
                at = 0
                for ref in dv_refs:
                    a, b = max(at, step * tile), min(at + ref.shape[0], (step + 1) * tile)
                    if a < b:
                        ref[a - at : b - at, :] = dv[a - step * tile : b - step * tile, :]
                    at += ref.shape[0]

    du_ref[...] += product(g, v, TN)


def returns_kernel(tile, scal_ref, hi_ref, lo_ref, caption_ref, after_ref, g_hi_ref, g_lo_ref, v_hi_ref, v_lo_ref, *dv_refs):
    del after_ref
    t = pl.program_id(0)
    u = (hi_ref[...], lo_ref[...])
    v = split(unit(caption_ref[...]))
    v_hi_ref[...], v_lo_ref[...] = v
    g = weights(u, v, scal_ref)
    g_hi_ref[...], g_lo_ref[...] = g
    dv = product(g, u, NN)
    for step in range(sum(ref.shape[0] for ref in dv_refs) // tile):

        @pl.when(t == step)
        def _():
            at = 0
            for ref in dv_refs:
                a, b = max(at, step * tile), min(at + ref.shape[0], (step + 1) * tile)
                if a < b:
                    ref[a - at : b - at, :] = dv[a - step * tile : b - step * tile, :]
                at += ref.shape[0]


def rest_kernel(g_hi_ref, g_lo_ref, v_hi_ref, v_lo_ref, du_ref, image_ref, grad_ref):
    du = du_ref[...] + product((g_hi_ref[...], g_lo_ref[...]), (v_hi_ref[...], v_lo_ref[...]), TN)
    grad_ref[...] = projected(image_ref[...], du)


def images_kernel(scal_ref, u_ref, caption_ref, dv_in_ref, after_ref, dv_ref, hi_ref, lo_ref):
    del after_ref

    @pl.when(pl.program_id(0) == 0)
    def _():
        hi_ref[...], lo_ref[...] = split(u_ref[...])

    u = (hi_ref[...], lo_ref[...])
    g = weights(u, split(unit(caption_ref[...])), scal_ref)
    dv_ref[...] = dv_in_ref[...] + product(g, u, NN)


def finish_kernel(caption_ref, base_ref, part_ref, *rest):
    rest[-1][...] = projected(caption_ref[...], base_ref[...] + part_ref[...])


def ready_kernel(caption_ref, base_ref, one_ref, r_ref, done_ref):
    raw = caption_ref[...]
    r = 1.0 / norm_of(raw)
    one_ref[...] = raw * r
    r_ref[...] = jnp.broadcast_to(r, r_ref.shape)
    done_ref[...] = projected(raw, base_ref[...])


def end_kernel(at, one_ref, r_ref, done_ref, part_ref, grad_in_ref, grad_ref, out_ref, sem):
    del grad_in_ref
    one, part = one_ref[...], part_ref[...]
    out_ref[...] = done_ref[...] + (part - one * jnp.sum(one * part, axis=-1, keepdims=True)) * r_ref[:, :1]
    copy = pltpu.make_async_copy(out_ref, grad_ref.at[pl.ds(at, out_ref.shape[0]), :], sem)
    copy.start()
    copy.wait()


def whole(shape):
    return pl.BlockSpec(shape, lambda t: (0,) * len(shape), pipeline_mode=pl.Buffered(1))


def result(shape):
    return pl.BlockSpec(shape, lambda t: (0,) * len(shape))


def blocks(tile, d, first=0):
    return pl.BlockSpec((tile, d), lambda t: (t + first, 0))


def shape(rows, d, dtype=F32):
    return jax.ShapeDtypeStruct((rows, d), dtype)


def halves(rows, d):
    return [pltpu.VMEM((rows, d), jnp.bfloat16)] * 2


def cost(products, rows, cols, d, scale=1.0):
    return pl.CostEstimate(flops=int(scale * 2 * 3 * products * rows * cols * d), bytes_accessed=16 * rows * d, transcendentals=rows * cols)


def own_block(first, scal, ids, image, caption, after):
    rows, d = image.shape
    return pl.pallas_call(
        own_kernel,
        grid=(rows // TILE,),
        in_specs=[SMEM, SMEM, whole((1, rows)), whole((rows, d)), blocks(TILE, d), pl.BlockSpec(memory_space=pl.ANY)],
        out_specs=[result((rows, d))] * 4 + [blocks(TILE, d)],
        out_shape=[shape(rows, d)] + [shape(rows, d, jnp.bfloat16)] * 2 + [shape(rows, d)] * 2,
        compiler_params=PARAMS,
        cost_estimate=cost(3, rows, rows, d, SCALE['own']),
        name="own",
    )(first, scal, ids, image, caption, after)


def score(scal, u, chunks, du, pieces, name, passed=None):
    rows, d = du.shape
    part = sum(c.shape[0] for c in chunks)
    tile = max(c for c in range(16, TILE + 128, 16) if part % c == 0)
    extra = [] if passed is None else [passed]
    kept = [pl.BlockSpec(memory_space=pl.ANY)] * len(extra)
    return pl.pallas_call(
        functools.partial(score_kernel, len(chunks), len(extra), tile),
        grid=(part // tile,),
        in_specs=[SMEM] + [whole((rows, d))] * 2 + [whole(c.shape) for c in chunks] + [whole((rows, d))] + kept,
        out_specs=[result((rows, d))] + kept + [result((n, d)) for n in pieces],
        out_shape=[shape(rows, d)] + [shape(*x.shape) for x in extra] + [shape(n, d) for n in pieces],
        scratch_shapes=halves(part, d),
        input_output_aliases={4 + len(chunks): 1} if extra else {},
        compiler_params=PARAMS,
        cost_estimate=cost(3 if pieces else 2, part, rows, d, SCALE[name]),
        name=name,
    )(scal, *u, *chunks, du, *extra)


def cycle_images(scal, u, caption, dv, after):
    rows, d = dv.shape
    return pl.pallas_call(
        images_kernel,
        grid=(rows // TILE,),
        in_specs=[SMEM, whole((rows, d)), blocks(TILE, d), blocks(TILE, d), pl.BlockSpec(memory_space=pl.ANY)],
        out_specs=blocks(TILE, d),
        out_shape=shape(rows, d),
        scratch_shapes=halves(rows, d),
        compiler_params=PARAMS,
        cost_estimate=cost(2, rows, rows, d),
        name="cyc_images",
    )(scal, u, caption, dv, after)


def returns(scal, u, captions, pieces, after):
    rows, d = u[0].shape
    part = captions.shape[0]
    tile = max(c for c in range(16, TILE + 128, 16) if part % c == 0)
    out = [(part, rows)] * 2 + [(part, d)] * 2
    return pl.pallas_call(
        functools.partial(returns_kernel, tile),
        grid=(part // tile,),
        in_specs=[SMEM] + [whole((rows, d))] * 2 + [blocks(tile, d), pl.BlockSpec(memory_space=pl.ANY)],
        out_specs=[blocks(tile, c) for _, c in out] + [result((n, d)) for n in pieces],
        out_shape=[shape(n, c, jnp.bfloat16) for n, c in out] + [shape(n, d) for n in pieces],
        compiler_params=PARAMS,
        cost_estimate=cost(2, part, rows, d, SCALE["part_b"]),
        name="part_b",
    )(scal, *u, captions, after)


def image_gradient(g, v, du, image):
    rows, d = du.shape
    part = v[0].shape[0]
    return pl.pallas_call(
        rest_kernel,
        grid=(rows // TILE,),
        in_specs=[pl.BlockSpec((part, TILE), lambda t: (0, t))] * 2 + [whole((part, d))] * 2 + [blocks(TILE, d)] * 2,
        out_specs=blocks(TILE, d),
        out_shape=shape(rows, d),
        compiler_params=PARAMS,
        cost_estimate=cost(1, part, rows, d, SCALE["rest"]),
        name="image_grad",
    )(*g, *v, du, image)


def finish(caption, base, part, at, grad=None):
    rows, d = caption.shape
    n = part.shape[0]
    tile = max(c for c in range(8, 200, 8) if n % c == 0 and at % c == 0)
    more = grad is not None
    return pl.pallas_call(
        finish_kernel,
        grid=(n // tile,),
        in_specs=[blocks(tile, d, at // tile)] * 2 + [blocks(tile, d)] + [pl.BlockSpec(memory_space=pl.ANY)] * more,
        out_specs=blocks(tile, d, at // tile),
        out_shape=shape(rows, d),
        input_output_aliases={3: 0} if more else {},
        compiler_params=SMALL,
        cost_estimate=pl.CostEstimate(flops=10 * part.size, bytes_accessed=16 * part.size, transcendentals=0),
        name="finish",
    )(caption, base, part, *([grad] if more else []))


def end(caption, base, part, at, grad):
    rows, d = caption.shape
    n = part.shape[0]
    one, r, done = pl.pallas_call(
        ready_kernel,
        grid=(1,),
        in_specs=[blocks(n, d, at // n)] * 2,
        out_specs=[blocks(n, d), blocks(n, 128), blocks(n, d)],
        out_shape=[shape(n, d), shape(n, 128), shape(n, d)],
        compiler_params=SMALL,
        cost_estimate=pl.CostEstimate(flops=10 * part.size, bytes_accessed=16 * part.size, transcendentals=0),
        name="ready",
    )(caption, base)
    local, anywhere = pl.BlockSpec(memory_space=pltpu.VMEM), pl.BlockSpec(memory_space=pl.ANY)
    return pl.pallas_call(
        functools.partial(end_kernel, at),
        in_specs=[local] * 4 + [anywhere],
        out_specs=anywhere,
        out_shape=shape(rows, d),
        scratch_shapes=[pltpu.VMEM((n, d), F32), pltpu.SemaphoreType.DMA],
        input_output_aliases={4: 0},
        compiler_params=SMALL,
        cost_estimate=pl.CostEstimate(flops=10 * part.size, bytes_accessed=16 * part.size, transcendentals=0),
        name="end",
    )(one, r, done, part, grad)


def body(image_embed, caption_embed, pair_ids, log_scale, logit_bias):
    rows = image_embed.shape[0]
    chunks, later = [], caption_embed
    for a, b in zip((0,) + CUTS, CUTS + (rows,)):
        chunk, later = lax.optimization_barrier((later[a:b], later))
        chunks.append(chunk)
    parts = [partner(c, "grp") for c in chunks]
    cycles = [passed_along(c, "blk", 1) for c in chunks]
    scal = jnp.concatenate([jnp.exp(log_scale), logit_bias])
    first = (lax.axis_index("grp") * lax.axis_size("blk") + lax.axis_index("blk")) * rows
    one, hi, lo, du, dv = own_block(first.astype(jnp.int32)[None], scal, pair_ids[None, :], image_embed, caption_embed, parts[0])
    u = (hi, lo)
    du, one, dv_part0 = score(scal, u, parts[:-1], du, [CUTS[-1]], "part_a", one)
    back0 = partner(dv_part0, "grp")
    next_u = passed_along(one, "blk", -1)
    (du,) = score(scal, u, cycles, du, [], "cyc_captions")
    edges = CUTS[-1:] + BACK + (rows,)
    pieces = [b - a for a, b in zip(edges, edges[1:])]
    g_hi, g_lo, v_hi, v_lo, *dv_part1 = returns(scal, u, parts[-1], pieces, du)
    backs = [partner(piece, "grp") for piece in dv_part1]
    image_grad = image_gradient((g_hi, g_lo), (v_hi, v_lo), du, image_embed)
    base = cycle_images(scal, next_u, caption_embed, dv, image_grad)
    grad = finish(caption_embed, base, back0, 0)
    for at, back in zip(edges[:-2], backs):
        grad = finish(caption_embed, base, back, at, grad)
    grad = end(caption_embed, base, backs[-1], edges[-2], grad)
    return (image_grad, grad)


def solution(mesh):
    in_specs = (P(("grp", "blk"), None), P(("grp", "blk"), None), P(("grp", "blk")), P(), P())
    out_specs = (P(("grp", "blk"), None), P(("grp", "blk"), None))
    return jax.shard_map(body, mesh=mesh, in_specs=in_specs, out_specs=out_specs, check_vma=False)
```

```python
import functools

import jax
import jax.numpy as jnp
from jax import lax
from jax.experimental import pallas as pl
from jax.experimental.pallas import tpu as pltpu
from jax.sharding import PartitionSpec as P

EPS = 1e-06
TILE = 256
VMEM = 50
CUTS = (128, 384)
SCALE = dict(own=1.0, part_a=1.0, cyc_captions=1.0, part_b=3.0, rest=2.0)
BACK = (768, 960)
NT = (((1,), (1,)), ((), ()))
NN = (((1,), (0,)), ((), ()))
TN = (((0,), (0,)), ((), ()))
F32 = jnp.float32
SMEM = pl.BlockSpec(memory_space=pltpu.SMEM)
PARAMS = pltpu.CompilerParams(vmem_limit_bytes=VMEM * 1024 * 1024)
SMALL = pltpu.CompilerParams(vmem_limit_bytes=12 * 1024 * 1024)


def passed_along(block, axis, distance):
    n = lax.axis_size(axis)
    return lax.ppermute(block, axis, [((i - distance) % n, i) for i in range(n)])


def partner(block, axis):
    n = lax.axis_size(axis)
    return lax.ppermute(block, axis, [(i, (i + n // 2) % n) for i in range(n)])


def split(x):
    hi = x.astype(jnp.bfloat16)
    lo = (x - hi.astype(F32)).astype(jnp.bfloat16)
    return hi, lo


def product(a, b, dims):
    dot = functools.partial(lax.dot_general, dimension_numbers=dims, preferred_element_type=F32)
    return dot(a[0], b[0]) + (dot(a[0], b[1]) + dot(a[1], b[0]))


def norm_of(x):
    return jnp.sqrt(jnp.sum(x * x, axis=-1, keepdims=True) + EPS)


def unit(x):
    return x * (1.0 / norm_of(x))


def projected(raw, grad):
    r = 1.0 / norm_of(raw)
    one = raw * r
    return (grad - one * jnp.sum(one * grad, axis=-1, keepdims=True)) * r


def weights(u, v, scal_ref, labels=None):
    weight = jax.nn.sigmoid(scal_ref[0] * product(v, u, NT) + scal_ref[1])
    if labels is not None:
        weight = weight - labels
    return split(scal_ref[0] * weight)


def cut_kernel(at, x_ref, out_ref, sem):
    copy = pltpu.make_async_copy(x_ref.at[pl.ds(at, out_ref.shape[0]), :], out_ref, sem)
    copy.start()
    copy.wait()


def own_kernel(first_ref, scal_ref, ids_ref, image_ref, caption_ref, after_ref, u_ref, hi_ref, lo_ref, du_ref, dv_ref):
    del after_ref
    t = pl.program_id(0)
    tile = caption_ref.shape[0]

    @pl.when(t == 0)
    def _():
        u = unit(image_ref[...])
        u_ref[...] = u
        hi_ref[...], lo_ref[...] = split(u)
        du_ref[...] = jnp.zeros_like(du_ref)

    columns = first_ref[0] + t * tile + lax.broadcasted_iota(jnp.int32, (tile, ids_ref.shape[1]), 0)
    labels = (ids_ref[...] == columns).astype(F32)
    u = (hi_ref[...], lo_ref[...])
    v = split(unit(caption_ref[...]))
    g = weights(u, v, scal_ref, labels)
    dv_ref[...] = product(g, u, NN)
    du_ref[...] += product(g, v, TN)


def score_kernel(chunks, passed, tile, scal_ref, hi_ref, lo_ref, *rest):
    caption_refs, du_in_ref, du_ref = rest[:chunks], rest[chunks], rest[chunks + 1 + passed]
    dv_refs, (v_hi_ref, v_lo_ref) = rest[chunks + 2 + 2 * passed : -2], rest[-2:]
    t = pl.program_id(0)

    @pl.when(t == 0)
    def _():
        at = 0
        for ref in caption_refs:
            n = ref.shape[0]
            v_hi_ref[at : at + n, :], v_lo_ref[at : at + n, :] = split(unit(ref[...]))
            at += n
        du_ref[...] = du_in_ref[...]

    rows = pl.ds(pl.multiple_of(t * tile, 16), tile)
    u = (hi_ref[...], lo_ref[...])
    v = (v_hi_ref[rows, :], v_lo_ref[rows, :])
    g = weights(u, v, scal_ref)
    if dv_refs:
        dv = product(g, u, NN)
        for step in range(v_hi_ref.shape[0] // tile):

            @pl.when(t == step)
            def _():
                at = 0
                for ref in dv_refs:
                    a, b = max(at, step * tile), min(at + ref.shape[0], (step + 1) * tile)
                    if a < b:
                        ref[a - at : b - at, :] = dv[a - step * tile : b - step * tile, :]
                    at += ref.shape[0]

    du_ref[...] += product(g, v, TN)


def returns_kernel(tile, scal_ref, hi_ref, lo_ref, caption_ref, after_ref, g_hi_ref, g_lo_ref, v_hi_ref, v_lo_ref, *dv_refs):
    del after_ref
    t = pl.program_id(0)
    u = (hi_ref[...], lo_ref[...])
    v = split(unit(caption_ref[...]))
    v_hi_ref[...], v_lo_ref[...] = v
    g = weights(u, v, scal_ref)
    g_hi_ref[...], g_lo_ref[...] = g
    dv = product(g, u, NN)
    for step in range(sum(ref.shape[0] for ref in dv_refs) // tile):

        @pl.when(t == step)
        def _():
            at = 0
            for ref in dv_refs:
                a, b = max(at, step * tile), min(at + ref.shape[0], (step + 1) * tile)
                if a < b:
                    ref[a - at : b - at, :] = dv[a - step * tile : b - step * tile, :]
                at += ref.shape[0]


def rest_kernel(g_hi_ref, g_lo_ref, v_hi_ref, v_lo_ref, du_ref, image_ref, grad_ref):
    du = du_ref[...] + product((g_hi_ref[...], g_lo_ref[...]), (v_hi_ref[...], v_lo_ref[...]), TN)
    grad_ref[...] = projected(image_ref[...], du)


def images_kernel(scal_ref, u_ref, caption_ref, dv_in_ref, after_ref, dv_ref, hi_ref, lo_ref):
    del after_ref

    @pl.when(pl.program_id(0) == 0)
    def _():
        hi_ref[...], lo_ref[...] = split(u_ref[...])

    u = (hi_ref[...], lo_ref[...])
    g = weights(u, split(unit(caption_ref[...])), scal_ref)
    dv_ref[...] = dv_in_ref[...] + product(g, u, NN)


def finish_kernel(caption_ref, base_ref, part_ref, *rest):
    rest[-1][...] = projected(caption_ref[...], base_ref[...] + part_ref[...])


def ready_kernel(caption_ref, base_ref, one_ref, r_ref, done_ref):
    raw = caption_ref[...]
    r = 1.0 / norm_of(raw)
    one_ref[...] = raw * r
    r_ref[...] = jnp.broadcast_to(r, r_ref.shape)
    done_ref[...] = projected(raw, base_ref[...])


def end_kernel(at, one_ref, r_ref, done_ref, part_ref, grad_in_ref, grad_ref, out_ref, sem):
    del grad_in_ref
    one, part = one_ref[...], part_ref[...]
    out_ref[...] = done_ref[...] + (part - one * jnp.sum(one * part, axis=-1, keepdims=True)) * r_ref[:, :1]
    copy = pltpu.make_async_copy(out_ref, grad_ref.at[pl.ds(at, out_ref.shape[0]), :], sem)
    copy.start()
    copy.wait()


def whole(shape):
    return pl.BlockSpec(shape, lambda t: (0,) * len(shape), pipeline_mode=pl.Buffered(1))


def result(shape):
    return pl.BlockSpec(shape, lambda t: (0,) * len(shape))


def blocks(tile, d, first=0):
    return pl.BlockSpec((tile, d), lambda t: (t + first, 0))


def shape(rows, d, dtype=F32):
    return jax.ShapeDtypeStruct((rows, d), dtype)


def halves(rows, d):
    return [pltpu.VMEM((rows, d), jnp.bfloat16)] * 2


def cost(products, rows, cols, d, scale=1.0):
    return pl.CostEstimate(flops=int(scale * 2 * 3 * products * rows * cols * d), bytes_accessed=16 * rows * d, transcendentals=rows * cols)


def cut(x, at, n):
    return pl.pallas_call(
        functools.partial(cut_kernel, at),
        in_specs=[pl.BlockSpec(memory_space=pltpu.HBM)],
        out_specs=pl.BlockSpec(memory_space=pltpu.VMEM),
        out_shape=pltpu.VMEM((n, x.shape[1]), F32),
        scratch_shapes=[pltpu.SemaphoreType.DMA],
        compiler_params=pltpu.CompilerParams(vmem_limit_bytes=62 * 1024 * 1024),
        cost_estimate=pl.CostEstimate(flops=0, bytes_accessed=8 * n * x.shape[1], transcendentals=0),
        name="cut",
    )(x)


def own_block(first, scal, ids, image, caption, after):
    rows, d = image.shape
    return pl.pallas_call(
        own_kernel,
        grid=(rows // TILE,),
        in_specs=[SMEM, SMEM, whole((1, rows)), whole((rows, d)), blocks(TILE, d), pl.BlockSpec(memory_space=pl.ANY)],
        out_specs=[result((rows, d))] * 4 + [blocks(TILE, d)],
        out_shape=[shape(rows, d)] + [shape(rows, d, jnp.bfloat16)] * 2 + [shape(rows, d)] * 2,
        compiler_params=PARAMS,
        cost_estimate=cost(3, rows, rows, d, SCALE['own']),
        name="own",
    )(first, scal, ids, image, caption, after)


def score(scal, u, chunks, du, pieces, name, passed=None):
    rows, d = du.shape
    part = sum(c.shape[0] for c in chunks)
    tile = max(c for c in range(16, TILE + 128, 16) if part % c == 0)
    extra = [] if passed is None else [passed]
    kept = [pl.BlockSpec(memory_space=pl.ANY)] * len(extra)
    return pl.pallas_call(
        functools.partial(score_kernel, len(chunks), len(extra), tile),
        grid=(part // tile,),
        in_specs=[SMEM] + [whole((rows, d))] * 2 + [whole(c.shape) for c in chunks] + [whole((rows, d))] + kept,
        out_specs=[result((rows, d))] + kept + [result((n, d)) for n in pieces],
        out_shape=[shape(rows, d)] + [shape(*x.shape) for x in extra] + [shape(n, d) for n in pieces],
        scratch_shapes=halves(part, d),
        input_output_aliases={4 + len(chunks): 1} if extra else {},
        compiler_params=PARAMS,
        cost_estimate=cost(3 if pieces else 2, part, rows, d, SCALE[name]),
        name=name,
    )(scal, *u, *chunks, du, *extra)


def cycle_images(scal, u, caption, dv, after):
    rows, d = dv.shape
    return pl.pallas_call(
        images_kernel,
        grid=(rows // TILE,),
        in_specs=[SMEM, whole((rows, d)), blocks(TILE, d), blocks(TILE, d), pl.BlockSpec(memory_space=pl.ANY)],
        out_specs=blocks(TILE, d),
        out_shape=shape(rows, d),
        scratch_shapes=halves(rows, d),
        compiler_params=PARAMS,
        cost_estimate=cost(2, rows, rows, d),
        name="cyc_images",
    )(scal, u, caption, dv, after)


def returns(scal, u, captions, pieces, after):
    rows, d = u[0].shape
    part = captions.shape[0]
    tile = max(c for c in range(16, TILE + 128, 16) if part % c == 0)
    out = [(part, rows)] * 2 + [(part, d)] * 2
    return pl.pallas_call(
        functools.partial(returns_kernel, tile),
        grid=(part // tile,),
        in_specs=[SMEM] + [whole((rows, d))] * 2 + [blocks(tile, d), pl.BlockSpec(memory_space=pl.ANY)],
        out_specs=[blocks(tile, c) for _, c in out] + [result((n, d)) for n in pieces],
        out_shape=[shape(n, c, jnp.bfloat16) for n, c in out] + [shape(n, d) for n in pieces],
        compiler_params=PARAMS,
        cost_estimate=cost(2, part, rows, d, SCALE["part_b"]),
        name="part_b",
    )(scal, *u, captions, after)


def image_gradient(g, v, du, image):
    rows, d = du.shape
    part = v[0].shape[0]
    return pl.pallas_call(
        rest_kernel,
        grid=(rows // TILE,),
        in_specs=[pl.BlockSpec((part, TILE), lambda t: (0, t))] * 2 + [whole((part, d))] * 2 + [blocks(TILE, d)] * 2,
        out_specs=blocks(TILE, d),
        out_shape=shape(rows, d),
        compiler_params=PARAMS,
        cost_estimate=cost(1, part, rows, d, SCALE["rest"]),
        name="image_grad",
    )(*g, *v, du, image)


def finish(caption, base, part, at, grad=None):
    rows, d = caption.shape
    n = part.shape[0]
    tile = max(c for c in range(8, 200, 8) if n % c == 0 and at % c == 0)
    more = grad is not None
    return pl.pallas_call(
        finish_kernel,
        grid=(n // tile,),
        in_specs=[blocks(tile, d, at // tile)] * 2 + [blocks(tile, d)] + [pl.BlockSpec(memory_space=pl.ANY)] * more,
        out_specs=blocks(tile, d, at // tile),
        out_shape=shape(rows, d),
        input_output_aliases={3: 0} if more else {},
        compiler_params=SMALL,
        cost_estimate=pl.CostEstimate(flops=10 * part.size, bytes_accessed=16 * part.size, transcendentals=0),
        name="finish",
    )(caption, base, part, *([grad] if more else []))


def end(caption, base, part, at, grad):
    rows, d = caption.shape
    n = part.shape[0]
    one, r, done = pl.pallas_call(
        ready_kernel,
        grid=(1,),
        in_specs=[blocks(n, d, at // n)] * 2,
        out_specs=[blocks(n, d), blocks(n, 128), blocks(n, d)],
        out_shape=[shape(n, d), shape(n, 128), shape(n, d)],
        compiler_params=SMALL,
        cost_estimate=pl.CostEstimate(flops=10 * part.size, bytes_accessed=16 * part.size, transcendentals=0),
        name="ready",
    )(caption, base)
    local, anywhere = pl.BlockSpec(memory_space=pltpu.VMEM), pl.BlockSpec(memory_space=pl.ANY)
    return pl.pallas_call(
        functools.partial(end_kernel, at),
        in_specs=[local] * 4 + [anywhere],
        out_specs=anywhere,
        out_shape=shape(rows, d),
        scratch_shapes=[pltpu.VMEM((n, d), F32), pltpu.SemaphoreType.DMA],
        input_output_aliases={4: 0},
        compiler_params=SMALL,
        cost_estimate=pl.CostEstimate(flops=10 * part.size, bytes_accessed=16 * part.size, transcendentals=0),
        name="end",
    )(one, r, done, part, grad)


def body(image_embed, caption_embed, pair_ids, log_scale, logit_bias):
    rows = image_embed.shape[0]
    chunks = [cut(caption_embed, a, b - a) for a, b in zip((0,) + CUTS, CUTS)] + [caption_embed[CUTS[-1] :]]
    parts = [partner(c, "grp") for c in chunks]
    cycles = [passed_along(c, "blk", 1) for c in chunks]
    scal = jnp.concatenate([jnp.exp(log_scale), logit_bias])
    first = (lax.axis_index("grp") * lax.axis_size("blk") + lax.axis_index("blk")) * rows
    one, hi, lo, du, dv = own_block(first.astype(jnp.int32)[None], scal, pair_ids[None, :], image_embed, caption_embed, parts[0])
    u = (hi, lo)
    du, one, dv_part0 = score(scal, u, parts[:-1], du, [CUTS[-1]], "part_a", one)
    back0 = partner(dv_part0, "grp")
    next_u = passed_along(one, "blk", -1)
    (du,) = score(scal, u, cycles, du, [], "cyc_captions")
    edges = CUTS[-1:] + BACK + (rows,)
    pieces = [b - a for a, b in zip(edges, edges[1:])]
    g_hi, g_lo, v_hi, v_lo, *dv_part1 = returns(scal, u, parts[-1], pieces, du)
    backs = [partner(piece, "grp") for piece in dv_part1]
    image_grad = image_gradient((g_hi, g_lo), (v_hi, v_lo), du, image_embed)
    base = cycle_images(scal, next_u, caption_embed, dv, image_grad)
    grad = finish(caption_embed, base, back0, 0)
    for at, back in zip(edges[:-2], backs):
        grad = finish(caption_embed, base, back, at, grad)
    grad = end(caption_embed, base, backs[-1], edges[-2], grad)
    return (image_grad, grad)


def solution(mesh):
    in_specs = (P(("grp", "blk"), None), P(("grp", "blk"), None), P(("grp", "blk")), P(), P())
    out_specs = (P(("grp", "blk"), None), P(("grp", "blk"), None))
    return jax.shard_map(body, mesh=mesh, in_specs=in_specs, out_specs=out_specs, check_vma=False)
```

```python
import functools

import jax
import jax.numpy as jnp
from jax import lax
from jax.experimental import pallas as pl
from jax.experimental.pallas import tpu as pltpu
from jax.sharding import PartitionSpec as P

EPS = 1e-06
TILE = 256
VMEM = 50
CUTS = (96, 384)
SCALE = dict(own=1.0, part_a=1.0, cyc_captions=1.0, part_b=3.0, rest=2.0)
BACK = (768, 960)
NT = (((1,), (1,)), ((), ()))
NN = (((1,), (0,)), ((), ()))
TN = (((0,), (0,)), ((), ()))
F32 = jnp.float32
SMEM = pl.BlockSpec(memory_space=pltpu.SMEM)
PARAMS = pltpu.CompilerParams(vmem_limit_bytes=VMEM * 1024 * 1024)
SMALL = pltpu.CompilerParams(vmem_limit_bytes=12 * 1024 * 1024)


def passed_along(block, axis, distance):
    n = lax.axis_size(axis)
    return lax.ppermute(block, axis, [((i - distance) % n, i) for i in range(n)])


def partner(block, axis):
    n = lax.axis_size(axis)
    return lax.ppermute(block, axis, [(i, (i + n // 2) % n) for i in range(n)])


def split(x):
    hi = x.astype(jnp.bfloat16)
    lo = (x - hi.astype(F32)).astype(jnp.bfloat16)
    return hi, lo


def product(a, b, dims):
    dot = functools.partial(lax.dot_general, dimension_numbers=dims, preferred_element_type=F32)
    return dot(a[0], b[0]) + (dot(a[0], b[1]) + dot(a[1], b[0]))


def norm_of(x):
    return jnp.sqrt(jnp.sum(x * x, axis=-1, keepdims=True) + EPS)


def unit(x):
    return x * (1.0 / norm_of(x))


def projected(raw, grad):
    r = 1.0 / norm_of(raw)
    one = raw * r
    return (grad - one * jnp.sum(one * grad, axis=-1, keepdims=True)) * r


def weights(u, v, scal_ref, labels=None):
    weight = jax.nn.sigmoid(scal_ref[0] * product(v, u, NT) + scal_ref[1])
    if labels is not None:
        weight = weight - labels
    return split(scal_ref[0] * weight)


def own_kernel(first_ref, scal_ref, ids_ref, image_ref, caption_ref, after_ref, u_ref, hi_ref, lo_ref, du_ref, dv_ref):
    del after_ref
    t = pl.program_id(0)
    tile = caption_ref.shape[0]

    @pl.when(t == 0)
    def _():
        u = unit(image_ref[...])
        u_ref[...] = u
        hi_ref[...], lo_ref[...] = split(u)
        du_ref[...] = jnp.zeros_like(du_ref)

    columns = first_ref[0] + t * tile + lax.broadcasted_iota(jnp.int32, (tile, ids_ref.shape[1]), 0)
    labels = (ids_ref[...] == columns).astype(F32)
    u = (hi_ref[...], lo_ref[...])
    v = split(unit(caption_ref[...]))
    g = weights(u, v, scal_ref, labels)
    dv_ref[...] = product(g, u, NN)
    du_ref[...] += product(g, v, TN)


def score_kernel(chunks, passed, tile, scal_ref, hi_ref, lo_ref, *rest):
    caption_refs, du_in_ref, du_ref = rest[:chunks], rest[chunks], rest[chunks + 1 + passed]
    dv_refs, (v_hi_ref, v_lo_ref) = rest[chunks + 2 + 2 * passed : -2], rest[-2:]
    t = pl.program_id(0)

    @pl.when(t == 0)
    def _():
        at = 0
        for ref in caption_refs:
            n = ref.shape[0]
            v_hi_ref[at : at + n, :], v_lo_ref[at : at + n, :] = split(unit(ref[...]))
            at += n
        du_ref[...] = du_in_ref[...]

    rows = pl.ds(pl.multiple_of(t * tile, 16), tile)
    u = (hi_ref[...], lo_ref[...])
    v = (v_hi_ref[rows, :], v_lo_ref[rows, :])
    g = weights(u, v, scal_ref)
    if dv_refs:
        dv = product(g, u, NN)
        for step in range(v_hi_ref.shape[0] // tile):

            @pl.when(t == step)
            def _():
                at = 0
                for ref in dv_refs:
                    a, b = max(at, step * tile), min(at + ref.shape[0], (step + 1) * tile)
                    if a < b:
                        ref[a - at : b - at, :] = dv[a - step * tile : b - step * tile, :]
                    at += ref.shape[0]

    du_ref[...] += product(g, v, TN)


def returns_kernel(tile, scal_ref, hi_ref, lo_ref, caption_ref, after_ref, g_hi_ref, g_lo_ref, v_hi_ref, v_lo_ref, *dv_refs):
    del after_ref
    t = pl.program_id(0)
    u = (hi_ref[...], lo_ref[...])
    v = split(unit(caption_ref[...]))
    v_hi_ref[...], v_lo_ref[...] = v
    g = weights(u, v, scal_ref)
    g_hi_ref[...], g_lo_ref[...] = g
    dv = product(g, u, NN)
    for step in range(sum(ref.shape[0] for ref in dv_refs) // tile):

        @pl.when(t == step)
        def _():
            at = 0
            for ref in dv_refs:
                a, b = max(at, step * tile), min(at + ref.shape[0], (step + 1) * tile)
                if a < b:
                    ref[a - at : b - at, :] = dv[a - step * tile : b - step * tile, :]
                at += ref.shape[0]


def rest_kernel(g_hi_ref, g_lo_ref, v_hi_ref, v_lo_ref, du_ref, image_ref, grad_ref):
    du = du_ref[...] + product((g_hi_ref[...], g_lo_ref[...]), (v_hi_ref[...], v_lo_ref[...]), TN)
    grad_ref[...] = projected(image_ref[...], du)


def images_kernel(scal_ref, u_ref, caption_ref, dv_in_ref, after_ref, dv_ref, hi_ref, lo_ref):
    del after_ref

    @pl.when(pl.program_id(0) == 0)
    def _():
        hi_ref[...], lo_ref[...] = split(u_ref[...])

    u = (hi_ref[...], lo_ref[...])
    g = weights(u, split(unit(caption_ref[...])), scal_ref)
    dv_ref[...] = dv_in_ref[...] + product(g, u, NN)


def finish_kernel(caption_ref, base_ref, part_ref, *rest):
    rest[-1][...] = projected(caption_ref[...], base_ref[...] + part_ref[...])


def ready_kernel(caption_ref, base_ref, one_ref, r_ref, done_ref):
    raw = caption_ref[...]
    r = 1.0 / norm_of(raw)
    one_ref[...] = raw * r
    r_ref[...] = jnp.broadcast_to(r, r_ref.shape)
    done_ref[...] = projected(raw, base_ref[...])


def end_kernel(at, one_ref, r_ref, done_ref, part_ref, grad_in_ref, grad_ref, out_ref, sem):
    del grad_in_ref
    one, part = one_ref[...], part_ref[...]
    out_ref[...] = done_ref[...] + (part - one * jnp.sum(one * part, axis=-1, keepdims=True)) * r_ref[:, :1]
    copy = pltpu.make_async_copy(out_ref, grad_ref.at[pl.ds(at, out_ref.shape[0]), :], sem)
    copy.start()
    copy.wait()


def whole(shape):
    return pl.BlockSpec(shape, lambda t: (0,) * len(shape), pipeline_mode=pl.Buffered(1))


def result(shape):
    return pl.BlockSpec(shape, lambda t: (0,) * len(shape))


def blocks(tile, d, first=0):
    return pl.BlockSpec((tile, d), lambda t: (t + first, 0))


def shape(rows, d, dtype=F32):
    return jax.ShapeDtypeStruct((rows, d), dtype)


def halves(rows, d):
    return [pltpu.VMEM((rows, d), jnp.bfloat16)] * 2


def cost(products, rows, cols, d, scale=1.0):
    return pl.CostEstimate(flops=int(scale * 2 * 3 * products * rows * cols * d), bytes_accessed=16 * rows * d, transcendentals=rows * cols)


def own_block(first, scal, ids, image, caption, after):
    rows, d = image.shape
    return pl.pallas_call(
        own_kernel,
        grid=(rows // TILE,),
        in_specs=[SMEM, SMEM, whole((1, rows)), whole((rows, d)), blocks(TILE, d), pl.BlockSpec(memory_space=pl.ANY)],
        out_specs=[result((rows, d))] * 4 + [blocks(TILE, d)],
        out_shape=[shape(rows, d)] + [shape(rows, d, jnp.bfloat16)] * 2 + [shape(rows, d)] * 2,
        compiler_params=PARAMS,
        cost_estimate=cost(3, rows, rows, d, SCALE['own']),
        name="own",
    )(first, scal, ids, image, caption, after)


def score(scal, u, chunks, du, pieces, name, passed=None):
    rows, d = du.shape
    part = sum(c.shape[0] for c in chunks)
    tile = max(c for c in range(16, TILE + 128, 16) if part % c == 0)
    extra = [] if passed is None else [passed]
    kept = [pl.BlockSpec(memory_space=pl.ANY)] * len(extra)
    return pl.pallas_call(
        functools.partial(score_kernel, len(chunks), len(extra), tile),
        grid=(part // tile,),
        in_specs=[SMEM] + [whole((rows, d))] * 2 + [whole(c.shape) for c in chunks] + [whole((rows, d))] + kept,
        out_specs=[result((rows, d))] + kept + [result((n, d)) for n in pieces],
        out_shape=[shape(rows, d)] + [shape(*x.shape) for x in extra] + [shape(n, d) for n in pieces],
        scratch_shapes=halves(part, d),
        input_output_aliases={4 + len(chunks): 1} if extra else {},
        compiler_params=PARAMS,
        cost_estimate=cost(3 if pieces else 2, part, rows, d, SCALE[name]),
        name=name,
    )(scal, *u, *chunks, du, *extra)


def cycle_images(scal, u, caption, dv, after):
    rows, d = dv.shape
    return pl.pallas_call(
        images_kernel,
        grid=(rows // TILE,),
        in_specs=[SMEM, whole((rows, d)), blocks(TILE, d), blocks(TILE, d), pl.BlockSpec(memory_space=pl.ANY)],
        out_specs=blocks(TILE, d),
        out_shape=shape(rows, d),
        scratch_shapes=halves(rows, d),
        compiler_params=PARAMS,
        cost_estimate=cost(2, rows, rows, d),
        name="cyc_images",
    )(scal, u, caption, dv, after)


def returns(scal, u, captions, pieces, after):
    rows, d = u[0].shape
    part = captions.shape[0]
    tile = max(c for c in range(16, TILE + 128, 16) if part % c == 0)
    out = [(part, rows)] * 2 + [(part, d)] * 2
    return pl.pallas_call(
        functools.partial(returns_kernel, tile),
        grid=(part // tile,),
        in_specs=[SMEM] + [whole((rows, d))] * 2 + [blocks(tile, d), pl.BlockSpec(memory_space=pl.ANY)],
        out_specs=[blocks(tile, c) for _, c in out] + [result((n, d)) for n in pieces],
        out_shape=[shape(n, c, jnp.bfloat16) for n, c in out] + [shape(n, d) for n in pieces],
        compiler_params=PARAMS,
        cost_estimate=cost(2, part, rows, d, SCALE["part_b"]),
        name="part_b",
    )(scal, *u, captions, after)


def image_gradient(g, v, du, image):
    rows, d = du.shape
    part = v[0].shape[0]
    return pl.pallas_call(
        rest_kernel,
        grid=(rows // TILE,),
        in_specs=[pl.BlockSpec((part, TILE), lambda t: (0, t))] * 2 + [whole((part, d))] * 2 + [blocks(TILE, d)] * 2,
        out_specs=blocks(TILE, d),
        out_shape=shape(rows, d),
        compiler_params=PARAMS,
        cost_estimate=cost(1, part, rows, d, SCALE["rest"]),
        name="image_grad",
    )(*g, *v, du, image)


def finish(caption, base, part, at, grad=None):
    rows, d = caption.shape
    n = part.shape[0]
    tile = max(c for c in range(8, 200, 8) if n % c == 0 and at % c == 0)
    more = grad is not None
    return pl.pallas_call(
        finish_kernel,
        grid=(n // tile,),
        in_specs=[blocks(tile, d, at // tile)] * 2 + [blocks(tile, d)] + [pl.BlockSpec(memory_space=pl.ANY)] * more,
        out_specs=blocks(tile, d, at // tile),
        out_shape=shape(rows, d),
        input_output_aliases={3: 0} if more else {},
        compiler_params=SMALL,
        cost_estimate=pl.CostEstimate(flops=10 * part.size, bytes_accessed=16 * part.size, transcendentals=0),
        name="finish",
    )(caption, base, part, *([grad] if more else []))


def end(caption, base, part, at, grad):
    rows, d = caption.shape
    n = part.shape[0]
    one, r, done = pl.pallas_call(
        ready_kernel,
        grid=(1,),
        in_specs=[blocks(n, d, at // n)] * 2,
        out_specs=[blocks(n, d), blocks(n, 128), blocks(n, d)],
        out_shape=[shape(n, d), shape(n, 128), shape(n, d)],
        compiler_params=SMALL,
        cost_estimate=pl.CostEstimate(flops=10 * part.size, bytes_accessed=16 * part.size, transcendentals=0),
        name="ready",
    )(caption, base)
    local, anywhere = pl.BlockSpec(memory_space=pltpu.VMEM), pl.BlockSpec(memory_space=pl.ANY)
    return pl.pallas_call(
        functools.partial(end_kernel, at),
        in_specs=[local] * 4 + [anywhere],
        out_specs=anywhere,
        out_shape=shape(rows, d),
        scratch_shapes=[pltpu.VMEM((n, d), F32), pltpu.SemaphoreType.DMA],
        input_output_aliases={4: 0},
        compiler_params=SMALL,
        cost_estimate=pl.CostEstimate(flops=10 * part.size, bytes_accessed=16 * part.size, transcendentals=0),
        name="end",
    )(one, r, done, part, grad)


def body(image_embed, caption_embed, pair_ids, log_scale, logit_bias):
    rows = image_embed.shape[0]
    chunks, later = [], caption_embed
    for a, b in zip((0,) + CUTS, CUTS + (rows,)):
        chunk, later = lax.optimization_barrier((later[a:b], later))
        chunks.append(chunk)
    parts = [partner(c, "grp") for c in chunks]
    cycles = [passed_along(c, "blk", 1) for c in chunks]
    scal = jnp.concatenate([jnp.exp(log_scale), logit_bias])
    first = (lax.axis_index("grp") * lax.axis_size("blk") + lax.axis_index("blk")) * rows
    one, hi, lo, du, dv = own_block(first.astype(jnp.int32)[None], scal, pair_ids[None, :], image_embed, caption_embed, parts[0])
    u = (hi, lo)
    du, one, dv_part0 = score(scal, u, parts[:-1], du, [CUTS[-1]], "part_a", one)
    back0 = partner(dv_part0, "grp")
    next_u = passed_along(one, "blk", -1)
    (du,) = score(scal, u, cycles, du, [], "cyc_captions")
    edges = CUTS[-1:] + BACK + (rows,)
    pieces = [b - a for a, b in zip(edges, edges[1:])]
    g_hi, g_lo, v_hi, v_lo, *dv_part1 = returns(scal, u, parts[-1], pieces, du)
    backs = [partner(piece, "grp") for piece in dv_part1]
    image_grad = image_gradient((g_hi, g_lo), (v_hi, v_lo), du, image_embed)
    base = cycle_images(scal, next_u, caption_embed, dv, image_grad)
    grad = finish(caption_embed, base, back0, 0)
    for at, back in zip(edges[:-2], backs):
        grad = finish(caption_embed, base, back, at, grad)
    grad = end(caption_embed, base, backs[-1], edges[-2], grad)
    return (image_grad, grad)


def solution(mesh):
    in_specs = (P(("grp", "blk"), None), P(("grp", "blk"), None), P(("grp", "blk")), P(), P())
    out_specs = (P(("grp", "blk"), None), P(("grp", "blk"), None))
    return jax.shard_map(body, mesh=mesh, in_specs=in_specs, out_specs=out_specs, check_vma=False)
```
